128 devices in a mesh: section: 4 (over y), tensor: 32 (over z, x, core).
Axes of the slice: x: 4, y: 4, z: 4, core: 2. Of those that a mesh axis runs over, the one named last changes fastest.
Arguments:
- token_ids: int32 [4, 128], replicated, may hold values from 0 to 64127
- embedding: bfloat16 [64128, 8192], P('section', 'tensor'), may hold values from -6 to 6
- norm_gain: float32 [4, 8192], P('section'), may hold values from 0.1 to 1.9
- query_weight: bfloat16 [4, 8192, 8192], P('section', None, 'tensor'), may hold values from -0.0625 to 0.0625
- keyval_weight: bfloat16 [4, 8192, 2048], P('section', None, 'tensor'), may hold values from -0.0625 to 0.0625
- output_weight: bfloat16 [4, 8192, 8192], P('section', 'tensor'), may hold values from -0.0625 to 0.0625
- prefix_cache: bfloat16 [4, 128, 128, 2, 1024], P('section', 'tensor')
- prefix_lengths: int32 [128], P('tensor'), may hold values from 16 to 128, as said below
Outputs:
- answers: float32 [4, 128, 8192], P('section', 'tensor')
The draws below stay inside these ranges and needn't reach their ends.
Inputs may be any that keep to these rules, and one draw needn't show every extreme that they name: `prefix_lengths`: some row has exactly 128 live positions.
All inputs are finite; a program needn't handle non-finite values.
Results may differ from the reference program's by a relative error of at most 0.039.
Values may be sent and summed in bfloat16 or wider, within the bound.
No kernel may reach another device: no remote copies, remote signals or barrier semaphores. Data moves between devices by JAX's collectives and lax.ppermute only.
A program may use at most 128 MiB of HBM per device.

```python
import math
import jax
import jax.numpy as jnp
import numpy as np
from jax import lax

D = 8192
HEADS = 64
KVH = 8
HD = 128
VOCAB = 64128
MAXLEN = 128
STEPS = 4
ROWS = 128
LAYERS = 4
N_TENSOR = 32


def draw_prefix_cache(key, part):
    base_key = jax.random.fold_in(key, 0)
    array_shape = (LAYERS, ROWS, MAXLEN, 2, KVH * HD)
    values = jax.random.truncated_normal(base_key, -6.0, 6.0, array_shape, jnp.float32)
    return values.astype(jnp.bfloat16)


def draw_prefix_lengths(key, part):
    length_key, pick_key = jax.random.split(key)
    drawn = jax.random.randint(length_key, (ROWS,), MAXLEN // 8, MAXLEN + 1)
    chosen = jax.random.randint(pick_key, (), 0, ROWS)
    return jnp.where(jnp.arange(ROWS) == chosen, MAXLEN, drawn).astype(jnp.int32)


def plant(array, stream_key, low, largest):
    spot = [jax.random.randint(jax.random.fold_in(stream_key, axis), (), 0, length) for axis, length in enumerate(array.shape)]
    main_axis = array.shape.index(max(array.shape))
    neighbour = spot[:main_axis] + [(spot[main_axis] + 1) % array.shape[main_axis]] + spot[main_axis + 1:]
    return array.at[tuple(spot)].set(low).at[tuple(neighbour)].set(largest)


def block_scale(rng, dims, cuts, low, top_value):
    loudness, own = 1.0, jax.random.fold_in(rng, 6)
    for dim, blocks in cuts:
        steps = jnp.exp(jax.random.uniform(jax.random.fold_in(own, dim), (blocks,), jnp.float32, low / len(cuts), top_value / len(cuts)))
        loudness = loudness * jnp.repeat(steps, dims[dim] // blocks).reshape([-1 if axis == dim else 1 for axis in range(len(dims))])
    return loudness


def rank_bounds(number_of, skew):
    portions = [(1 << 20) // math.isqrt(standing ** skew) + 1 for standing in range(1, number_of + 1)]
    width = 1 + sum(portions) // (1 << 30)
    return np.cumsum(np.array([max(1, weight // width) for weight in portions]))


def ranked_ids(stream_key, shape, amount, slope):
    grid = rank_bounds(amount, slope)
    pick = jax.random.randint(jax.random.fold_in(stream_key, 1), shape, 0, int(grid[amount - 1]))
    rank = jnp.searchsorted(jnp.asarray(grid, jnp.int32), pick, side="right")
    return jax.random.permutation(jax.random.fold_in(stream_key, 2), amount)[rank].astype(jnp.int32)


def gaussian(rng, dims, scale, limit, cuts=(), kind=jnp.bfloat16):
    values = jax.random.normal(rng, dims, jnp.float32) * scale
    if len(cuts) > 0:
        values = block_scale(rng, dims, cuts, -0.22, 0.18) * values
    return jnp.clip(values, min=-limit, max=limit).astype(kind)


def setup_inputs(seed: int = 0) -> dict:
    splits = jax.random.split(jax.random.key(seed), 9)
    return {
        "token_ids": plant(ranked_ids(splits[0], (STEPS, ROWS), VOCAB, 2), jax.random.fold_in(splits[0], 3), 0, VOCAB - 1).astype(jnp.int32),
        "embedding": gaussian(splits[1], (VOCAB, D), 1.0, 6.0, ((0, 4), (1, 32))),
        "norm_gain": jnp.clip(1.0 + 0.18 * jax.random.normal(splits[2], (LAYERS, D), jnp.float32), 0.1, 1.9),
        "query_weight": gaussian(splits[3], (LAYERS, D, HEADS * HD), D ** -0.5, 0.0625, ((0, 4), (2, 32))),
        "keyval_weight": gaussian(splits[4], (LAYERS, D, 2 * KVH * HD), D ** -0.5, 0.0625, ((0, 4), (2, 32))),
        "output_weight": gaussian(splits[5], (LAYERS, HEADS * HD, D), (HEADS * HD) ** -0.5, 0.0625, ((0, 4), (1, 32))),
        "prefix_cache": draw_prefix_cache(jax.random.fold_in(splits[8], 71), 0),
        "prefix_lengths": draw_prefix_lengths(jax.random.fold_in(splits[8], 71), 0),
    }


NORM_EPSILON = 1e-05
ROPE_BASE = 500000.0

def rope_tables(positions, head_dim):
    half_dim = head_dim // 2
    frequency = ROPE_BASE ** (-(jnp.arange(half_dim, dtype=jnp.float32) * 2.0 / head_dim))
    angles = positions.astype(jnp.float32)[:, None] * frequency[None, :]
    cosine = jnp.concatenate([jnp.cos(angles), jnp.cos(angles)], axis=-1)
    sine_table = jnp.concatenate([jnp.sin(angles), jnp.sin(angles)], axis=-1)
    return (cosine, sine_table)

def rotate(vectors, cosine, sine_table):
    half_dim = vectors.shape[-1] // 2
    swapped = jnp.concatenate([-vectors[..., half_dim:], vectors[..., :half_dim]], axis=-1)
    return vectors * cosine[:, None, :] + swapped * sine_table[:, None, :]

def normalize(values, gain_vec):
    scaling = lax.rsqrt(lax.optimization_barrier(jnp.mean(values * values, axis=-1, keepdims=True)) + NORM_EPSILON)
    return (values * scaling * gain_vec).astype(jnp.bfloat16)

def attend(queries, prefix, fresh_rows, live_len, step_index):
    row_count, kv_heads, group_size, head_dim = queries.shape
    step_total = fresh_rows.shape[0]
    query_f = queries.astype(jnp.float32)
    past_keys = prefix[:, :, 0, :].reshape(row_count, -1, kv_heads, head_dim).astype(jnp.float32)
    past_vals = prefix[:, :, 1, :].reshape(row_count, -1, kv_heads, head_dim).astype(jnp.float32)
    new_keys = fresh_rows[:, :, 0, :].reshape(step_total, row_count, kv_heads, head_dim).astype(jnp.float32)
    new_vals = fresh_rows[:, :, 1, :].reshape(step_total, row_count, kv_heads, head_dim).astype(jnp.float32)
    score_scale = head_dim ** (-0.5)
    past_score = jnp.einsum('rkgd,rlkd->rkgl', query_f, past_keys) * score_scale
    new_score = jnp.einsum('rkgd,srkd->rkgs', query_f, new_keys) * score_scale
    past_mask = jnp.arange(past_keys.shape[1])[None, None, None, :] < live_len[:, None, None, None]
    new_mask = jnp.arange(step_total)[None, None, None, :] <= step_index
    past_score = jnp.where(past_mask, past_score, -1e+30)
    new_score = jnp.where(new_mask, new_score, -1e+30)
    top_score = jnp.maximum(lax.optimization_barrier(jnp.max(past_score, axis=-1)), lax.optimization_barrier(jnp.max(new_score, axis=-1)))[..., None]
    past_weight = jnp.exp(past_score - top_score)
    new_weight = jnp.exp(new_score - top_score)
    weight_total = lax.optimization_barrier(jnp.sum(past_weight, axis=-1, keepdims=True)) + lax.optimization_barrier(jnp.sum(new_weight, axis=-1, keepdims=True))
    past_prob = lax.optimization_barrier((past_weight / weight_total).astype(jnp.bfloat16)).astype(jnp.float32)
    new_prob = lax.optimization_barrier((new_weight / weight_total).astype(jnp.bfloat16)).astype(jnp.float32)
    attended = jnp.einsum('rkgl,rlkd->rkgd', past_prob, past_vals) + jnp.einsum('rkgs,srkd->rkgd', new_prob, new_vals)
    return attended.astype(jnp.bfloat16).reshape(row_count, kv_heads * group_size * head_dim)

def reference(token_ids, embedding, norm_gain, query_weight, keyval_weight, output_weight, prefix_cache, prefix_lengths):
    kv_width = KVH * HD
    group_size = HEADS // KVH
    part_width = HEADS * HD // N_TENSOR
    fresh_kv = jnp.zeros((LAYERS, STEPS, ROWS, 2, kv_width), jnp.bfloat16)
    outputs = []
    for step_index in range(STEPS):
        hidden = embedding[token_ids[step_index]].astype(jnp.float32)
        cosine, sine_table = rope_tables(prefix_lengths + step_index, HD)
        for layer_index in range(LAYERS):
            normed = normalize(hidden, norm_gain[layer_index])
            queries = jnp.dot(normed, query_weight[layer_index], preferred_element_type=jnp.float32)
            keyvals = jnp.dot(normed, keyval_weight[layer_index], preferred_element_type=jnp.float32)
            turned_q = rotate(queries.reshape(ROWS, HEADS, HD), cosine, sine_table).astype(jnp.bfloat16)
            turned_k = rotate(keyvals[:, :kv_width].reshape(ROWS, KVH, HD), cosine, sine_table).astype(jnp.bfloat16)
            value_cols = keyvals[:, kv_width:].astype(jnp.bfloat16)
            entry_kv = jnp.stack([turned_k.reshape(ROWS, kv_width), value_cols], axis=1)
            fresh_kv = fresh_kv.at[layer_index, step_index].set(entry_kv)
            mixed_out = attend(turned_q.reshape(ROWS, KVH, group_size, HD), prefix_cache[layer_index], fresh_kv[layer_index], prefix_lengths, step_index)
            summed = jnp.zeros((ROWS, D), jnp.float32)
            for shard_index in range(N_TENSOR):
                col_start = shard_index * part_width
                partial_term = jnp.dot(mixed_out[:, col_start:col_start + part_width], output_weight[layer_index, col_start:col_start + part_width], preferred_element_type=jnp.float32).astype(jnp.bfloat16)
                summed = summed + lax.optimization_barrier(partial_term).astype(jnp.float32)
            hidden = hidden + summed
        outputs.append(hidden)
    return jnp.stack(outputs)
```

```python
import jax
import jax.numpy as jnp
from jax import lax
from jax.sharding import PartitionSpec as P

HD = 128
NORM_EPSILON = 1e-05
ROPE_BASE = 500000.0
SECTIONS = 4
CHIPS = 16
CORES = 2
STEPS = 4
HEADS_PER_CHIP = 4
BF16 = jnp.bfloat16
F32 = jnp.float32
PLANE = [[2 * p + c for p in range(CHIPS)] for c in range(CORES)]


def section_send(block, distance):
    if distance == 0:
        return block
    route = [(i, (i + distance) % SECTIONS) for i in range(SECTIONS)]
    return lax.ppermute(block, "section", route)


def core_swap(block):
    return lax.ppermute(block, "tensor", [(i, i ^ 1) for i in range(CHIPS * CORES)])


def chip_send(block, target):
    route = [(2 * p + c, 2 * target(p) + c) for p in range(CHIPS) for c in range(CORES)]
    return lax.ppermute(block, "tensor", route)


def plane_exchange(blocks):
    return lax.all_to_all(
        blocks, "tensor", split_axis=0, concat_axis=0, tiled=True, axis_index_groups=PLANE
    )


def section_exchange(blocks):
    return lax.all_to_all(blocks, "section", split_axis=0, concat_axis=0, tiled=True)


def embed(token_ids, embedding, section_pos):
    vocab_part = embedding.shape[0]
    local_ids = token_ids.T.reshape(-1) - section_pos * vocab_part
    inside = (local_ids >= 0) & (local_ids < vocab_part)
    picked = jnp.take(embedding, jnp.clip(local_ids, 0, vocab_part - 1), axis=0)
    picked = jnp.where(inside[:, None], picked, jnp.zeros_like(picked))
    by_row = lax.all_to_all(
        picked.reshape(CHIPS * CORES, 16, -1), "tensor", split_axis=0, concat_axis=0, tiled=True
    )
    by_quarter = section_exchange(by_row).reshape(SECTIONS, 8, 16, -1)
    columns = jnp.sum(by_quarter.astype(F32), axis=0)
    return columns.transpose(1, 0, 2).reshape(16, -1)


def row_order(section_pos):
    place = jnp.arange(256)[:, None]
    source = jnp.arange(256)[None, :]
    turn, chip, step = place // 64, place // 4 % CHIPS, place % 4
    wanted = chip * 16 + (section_pos + turn) % SECTIONS * 4 + step
    forward = (wanted == source).astype(BF16)
    turn, chip, step = source // 64, source // 4 % CHIPS, source % 4
    held = chip * 16 + (section_pos - turn) % SECTIONS * 4 + step
    backward = (held == place).astype(BF16)
    return forward, backward


def project(rows, order, inverse_gain, weights):
    wq_mine, wq_other, keys_t, values_t = weights
    rows = jnp.dot(order, rows, preferred_element_type=F32).astype(BF16)
    plain = rows.astype(F32) * inverse_gain
    squares = jnp.sum(plain * plain, axis=-1, keepdims=True)
    transposed = (((1,), (1,)), ((), ()))
    parts = [
        jnp.dot(rows, wq_mine, preferred_element_type=F32),
        jnp.dot(rows, wq_other, preferred_element_type=F32),
        lax.dot_general(rows, keys_t, transposed, preferred_element_type=F32),
        lax.dot_general(rows, values_t, transposed, preferred_element_type=F32),
        jnp.broadcast_to(squares, (256, HD)),
    ]
    return jnp.concatenate(parts, axis=1)


def turn(vectors, cosine, sine):
    half = HD // 2
    swapped = jnp.concatenate([-vectors[..., half:], vectors[..., :half]], axis=-1)
    return vectors * cosine + swapped * sine


def attend(parts, cosine, sine, cache, lengths):
    total = (parts[0] + parts[1]) + (parts[2] + parts[3])
    width = HEADS_PER_CHIP * HD
    squares = total[:, width + 2 * HD : width + 2 * HD + 1]
    scaling = lax.rsqrt(squares / 8192.0 + NORM_EPSILON)
    total = total * scaling
    heads = [total[:, i * HD : (i + 1) * HD] for i in range(HEADS_PER_CHIP)]
    queries = jnp.concatenate([turn(h, cosine, sine) for h in heads], axis=0).astype(BF16)
    new_keys = turn(total[:, width : width + HD], cosine, sine).astype(BF16)
    new_values = total[:, width + HD : width + 2 * HD].astype(BF16)
    keys = cache[:, 0].reshape(-1, HD)
    values = cache[:, 1].reshape(-1, HD)
    transposed = (((1,), (1,)), ((), ()))
    scale = HD**-0.5
    past = lax.dot_general(queries, keys, transposed, preferred_element_type=F32) * scale
    new = lax.dot_general(queries, new_keys, transposed, preferred_element_type=F32) * scale
    row = jnp.arange(256)[:, None] % 64
    column = jnp.arange(past.shape[1])[None, :]
    live = lengths[:, None].repeat(HD, 1).reshape(1, -1)
    past_live = (row // 4 == column // 128) & (column % 128 < live)
    column = jnp.arange(64)[None, :]
    new_live = (row // 4 == column // 4) & (column % 4 <= row % 4)
    past = jnp.where(past_live, past, -1e30)
    new = jnp.where(new_live, new, -1e30)
    top = jnp.maximum(jnp.max(past, -1, keepdims=True), jnp.max(new, -1, keepdims=True))
    past = jnp.exp(past - top)
    new = jnp.exp(new - top)
    weight = jnp.sum(past, -1, keepdims=True) + jnp.sum(new, -1, keepdims=True)
    past = (past / weight).astype(BF16)
    new = (new / weight).astype(BF16)
    mixed = jnp.dot(past, values, preferred_element_type=F32)
    mixed = mixed + jnp.dot(new, new_values, preferred_element_type=F32)
    mixed = mixed.astype(BF16)
    return jnp.concatenate([mixed[i * 64 : (i + 1) * 64] for i in range(HEADS_PER_CHIP)], axis=1)


def body(
    token_ids,
    embedding,
    norm_gain,
    query_weight,
    keyval_weight,
    output_weight,
    prefix_cache,
    prefix_lengths,
):
    section_pos = lax.axis_index("section")
    tensor_pos = lax.axis_index("tensor")
    core, chip = tensor_pos % CORES, tensor_pos // CORES
    quarter = query_weight.shape[1] // SECTIONS

    def share(weight, axis, distance):
        start = (section_pos + distance) % SECTIONS * quarter
        return section_send(lax.dynamic_slice_in_dim(weight, start, quarter, axis), distance)

    kv_mat = keyval_weight[0].T
    wq_mine = [share(query_weight[0], 0, d) for d in range(SECTIONS)]
    kv_mine = jnp.stack([share(kv_mat, 1, d) for d in range(SECTIONS)])
    wo_mine = [share(output_weight[0], 1, d) for d in range(SECTIONS)]
    wq_other = jnp.stack([core_swap(w) for w in wq_mine])
    wo_other = jnp.stack([core_swap(w) for w in wo_mine])
    wq_mine = jnp.stack(wq_mine)
    wo_mine = jnp.stack(wo_mine)
    first = chip_send(kv_mine, lambda p: 2 * p if p < 8 else 2 * (p - 8) + 1)
    second = chip_send(kv_mine, lambda p: 2 * p + 1 if p < 8 else 2 * (p - 8))
    even = chip % 2 == 0
    heads_t = []
    for half in (jnp.where(even, first, second), jnp.where(even, second, first)):
        other = core_swap(half)
        low = jnp.where(core == 0, half, other)
        high = jnp.where(core == 0, other, half)
        heads_t.append(jnp.concatenate([low, high], axis=1))
    keys_t, values_t = heads_t

    gains = section_exchange(norm_gain[0].reshape(SECTIONS, quarter))
    hidden = embed(token_ids, embedding, section_pos)

    lengths = lax.all_gather(prefix_lengths, "tensor", axis=0, axis_index_groups=PLANE)
    lengths = lax.dynamic_index_in_dim(lengths, section_pos, 1, keepdims=False)
    cache = section_exchange(prefix_cache[0])
    cache = cache.reshape(SECTIONS, 128, 2, 8, HD).transpose(3, 0, 2, 1, 4)
    cache = plane_exchange(jnp.repeat(cache, 2, axis=0))

    frequency = ROPE_BASE ** (-(jnp.arange(HD // 2, dtype=F32) * 2.0 / HD))
    positions = (lengths[:, None] + jnp.arange(STEPS)[None, :]).reshape(-1).astype(F32)
    angles = positions[:, None] * frequency[None, :]
    cosine = jnp.concatenate([jnp.cos(angles)] * 2, axis=-1)
    sine = jnp.concatenate([jnp.sin(angles)] * 2, axis=-1)
    forward, backward = row_order(section_pos)

    for layer in range(SECTIONS):
        slot = (section_pos - layer) % SECTIONS
        pick = lambda stacked: lax.dynamic_index_in_dim(stacked, slot, 0, keepdims=False)
        gain = gains[layer][None, :]
        scaled = (hidden * gain).astype(BF16)
        rows = plane_exchange(jnp.broadcast_to(scaled[None], (CHIPS, 16, quarter)))
        weights = [pick(w) for w in (wq_mine, wq_other, keys_t, values_t)]
        partial = project(rows.reshape(256, quarter), forward, 1.0 / gain, weights)
        parts = [section_send(partial[64 * d : 64 * (d + 1)], d) for d in range(SECTIONS)]
        mixed = attend(parts, cosine, sine, cache[:, layer], lengths)
        gathered = jnp.concatenate([section_send(mixed, d) for d in range(SECTIONS)], axis=0)
        gathered = jnp.dot(backward, gathered, preferred_element_type=F32).astype(BF16)
        out_mat = jnp.concatenate([pick(wo_mine), pick(wo_other)], axis=0)
        terms = jnp.dot(gathered, out_mat, preferred_element_type=F32).astype(BF16)
        terms = plane_exchange(terms.reshape(CHIPS, 16, quarter))
        hidden = hidden + jnp.sum(terms.astype(F32), axis=0)

    finals = section_exchange(hidden.reshape(4, STEPS, quarter).transpose(1, 0, 2))
    return finals.transpose(1, 0, 2).reshape(1, 4, SECTIONS * quarter)


def solution(mesh):
    in_specs = (
        P(),
        P("section", "tensor"),
        P("section", None),
        P("section", None, "tensor"),
        P("section", None, "tensor"),
        P("section", "tensor", None),
        P("section", "tensor", None, None, None),
        P("tensor"),
    )
    out_specs = P("section", "tensor", None)
    return jax.shard_map(body, mesh=mesh, in_specs=in_specs, out_specs=out_specs, check_vma=False)
```

```python
import jax
import jax.numpy as jnp
from jax import lax
from jax.experimental import pallas as pl
from jax.experimental.pallas import tpu as pltpu
from jax.sharding import PartitionSpec as P

HD = 128
NORM_EPSILON = 1e-05
ROPE_BASE = 500000.0
SECTIONS = 4
CHIPS = 16
CORES = 2
STEPS = 4
HEADS_PER_CHIP = 4
BF16 = jnp.bfloat16
F32 = jnp.float32
PLANE = [[2 * p + c for p in range(CHIPS)] for c in range(CORES)]


def section_send(block, distance):
    if distance == 0:
        return block
    route = [(i, (i + distance) % SECTIONS) for i in range(SECTIONS)]
    return lax.ppermute(block, "section", route)


def core_swap(block):
    return lax.ppermute(block, "tensor", [(i, i ^ 1) for i in range(CHIPS * CORES)])


def chip_send(block, target):
    route = [(2 * p + c, 2 * target(p) + c) for p in range(CHIPS) for c in range(CORES)]
    return lax.ppermute(block, "tensor", route)


def plane_exchange(blocks):
    return lax.all_to_all(
        blocks, "tensor", split_axis=0, concat_axis=0, tiled=True, axis_index_groups=PLANE
    )


def section_exchange(blocks):
    return lax.all_to_all(blocks, "section", split_axis=0, concat_axis=0, tiled=True)


def in_three(values):
    high = lax.reduce_precision(values, 8, 7)
    middle = lax.reduce_precision(values - high, 8, 7)
    return [part.astype(BF16) for part in (high, middle, values - high - middle)]


def embed(token_ids, embedding, prefix_lengths, norm_gain, section_pos, core):
    vocab_part, width = embedding.shape
    local_ids = token_ids.T.reshape(-1) - section_pos * vocab_part
    inside = (local_ids >= 0) & (local_ids < vocab_part)
    picked = jnp.take(embedding, jnp.clip(local_ids, 0, vocab_part - 1), axis=0)
    picked = jnp.where(inside[:, None], picked, jnp.zeros_like(picked))
    picked = picked.reshape(CHIPS * CORES, 16, width)
    extra = jnp.pad(prefix_lengths.astype(BF16)[None, :], ((0, 7), (0, width - 4)))
    extra = jnp.broadcast_to(extra[None], (CHIPS * CORES, 8, width))
    by_row = lax.all_to_all(
        jnp.concatenate([picked, extra], axis=1), "tensor", split_axis=0, concat_axis=0, tiled=True
    )
    lengths = by_row[:, 16, :4].reshape(CHIPS, CORES, 4)
    lengths = lax.dynamic_index_in_dim(lengths, core, 1, keepdims=False)
    lengths = lax.dynamic_index_in_dim(lengths, section_pos, 1, keepdims=False)
    gains = jnp.stack(in_three(norm_gain.reshape(CHIPS * CORES, width)), axis=1)
    gains = jnp.pad(gains, ((0, 0), (0, 5), (0, 0)))
    by_quarter = section_exchange(jnp.concatenate([by_row[:, :16], gains], axis=1))
    by_quarter = by_quarter.reshape(SECTIONS, 8, 24, width).astype(F32)
    columns = jnp.sum(by_quarter[:, :, :16], axis=0).transpose(1, 0, 2).reshape(16, -1)
    gains = (by_quarter[:, :, 16] + by_quarter[:, :, 17]) + by_quarter[:, :, 18]
    return columns, gains.reshape(SECTIONS, 1, -1), lengths.astype(jnp.int32)


def row_orders(section_pos):
    place = jnp.arange(256)[:, None]
    source = jnp.arange(256)[None, :]
    wanted = place // 4 % CHIPS * 16 + place // 64 * 4 + place % 4
    forward = (wanted == source).astype(BF16)
    held = source // 4 % CHIPS * 16 + (section_pos - source // 64) % SECTIONS * 4 + source % 4
    backward = (held == place).astype(BF16)
    return forward, backward


TRANSPOSED = (((1,), (1,)), ((), ()))
WIDTH = HEADS_PER_CHIP * HD
SENT = WIDTH + 3 * HD


def project_kernel(rows, order, gain, wq_mine, wq_other, keys_t, values_t, out, total):
    step = pl.program_id(0)

    @pl.when(step == 0)
    def _():
        total[...] = jnp.zeros_like(total)

    block = rows[...].reshape(256, rows.shape[2])
    block = jnp.dot(order[...], block, preferred_element_type=F32).astype(BF16)
    plain = block.astype(F32) / gain[...]
    half = WIDTH // 2
    total[:, :half] += jnp.dot(block, wq_mine[...], preferred_element_type=F32)
    total[:, half:WIDTH] += jnp.dot(block, wq_other[...], preferred_element_type=F32)
    for start, weight in ((WIDTH, keys_t), (WIDTH + HD, values_t)):
        total[:, start : start + HD] += lax.dot_general(
            block, weight[...], TRANSPOSED, preferred_element_type=F32
        )
    total[:, WIDTH + 2 * HD :] += jnp.sum(plain * plain, axis=1, keepdims=True)

    @pl.when(step == pl.num_programs(0) - 1)
    def _():
        squares = total[:, WIDTH + 2 * HD :]
        high = squares.astype(BF16).astype(F32)
        middle = (squares - high).astype(BF16).astype(F32)
        low = squares - high - middle
        lane = lax.broadcasted_iota(jnp.int32, squares.shape, 1)
        parts = jnp.where(lane == 0, high, jnp.where(lane == 1, middle, low))
        parts = jnp.where(lane < 3, parts, 0.0)
        for j in range(SECTIONS):
            own = slice(64 * j, 64 * (j + 1))
            out[j, :, : WIDTH + 2 * HD] = total[own, : WIDTH + 2 * HD].astype(BF16)
            out[j, :, WIDTH + 2 * HD :] = parts[own].astype(BF16)


def project(rows, order, gain, layer, wq_mine, wq_other, keys_t, values_t):
    quarter = rows.shape[2]
    chunk = quarter // 4
    flops = 2 * 256 * quarter * (256 + WIDTH + 2 * HD)
    return pl.pallas_call(
        project_kernel,
        grid=(quarter // chunk,),
        in_specs=[
            pl.BlockSpec((CHIPS, 16, chunk), lambda k: (0, 0, k)),
            pl.BlockSpec((256, 256), lambda k: (0, 0)),
            pl.BlockSpec((None, 1, chunk), lambda k: (layer, 0, k)),
            pl.BlockSpec((None, chunk, 256), lambda k: (layer, k, 0)),
            pl.BlockSpec((None, chunk, 256), lambda k: (layer, k, 0)),
            pl.BlockSpec((None, HD, chunk), lambda k: (layer, 0, k)),
            pl.BlockSpec((None, HD, chunk), lambda k: (layer, 0, k)),
        ],
        out_specs=pl.BlockSpec((SECTIONS, 64, SENT), lambda k: (0, 0, 0)),
        out_shape=jax.ShapeDtypeStruct((SECTIONS, 64, SENT), BF16),
        scratch_shapes=[pltpu.VMEM((256, SENT), F32)],
        compiler_params=pltpu.CompilerParams(vmem_limit_bytes=32 * 2**20),
        cost_estimate=pl.CostEstimate(flops=flops, bytes_accessed=5 * 2**20, transcendentals=0),
        name="project",
    )(rows, order, gain, wq_mine, wq_other, keys_t, values_t)


def attend_kernel(parts, cosine, sine, bias, cache, out):
    total = parts[0].astype(F32)
    for i in range(1, SECTIONS):
        total = total + parts[i].astype(F32)
    squares = jnp.sum(total[:, WIDTH + 2 * HD :], axis=1, keepdims=True)
    scaling = lax.rsqrt(squares / 8192.0 + NORM_EPSILON)
    turned_cos = cosine[...] * scaling
    turned_sin = sine[...] * scaling

    def turn(vectors):
        half = HD // 2
        swapped = jnp.concatenate([-vectors[:, half:], vectors[:, :half]], axis=1)
        return (vectors * turned_cos + swapped * turned_sin).astype(BF16)

    queries = [turn(total[:, HD * h : HD * (h + 1)]) for h in range(HEADS_PER_CHIP)]
    new_keys = turn(total[:, WIDTH : WIDTH + HD])
    new_values = (total[:, WIDTH + HD : WIDTH + 2 * HD] * scaling).astype(BF16)
    row = lax.broadcasted_iota(jnp.int32, (64, 16), 0) % 16
    column = lax.broadcasted_iota(jnp.int32, (64, 16), 1)
    new_live = (row // 4 == column // 4) & (column % 4 <= row % 4)
    scale = HD**-0.5
    for g in range(4):
        own = slice(16 * g, 16 * (g + 1))
        query = jnp.concatenate([q[own] for q in queries], axis=0)
        keys = cache[4 * g : 4 * (g + 1), 0].reshape(4 * 128, HD)
        values = cache[4 * g : 4 * (g + 1), 1].reshape(4 * 128, HD)
        past = lax.dot_general(query, keys, TRANSPOSED, preferred_element_type=F32) * scale
        new = lax.dot_general(query, new_keys[own], TRANSPOSED, preferred_element_type=F32) * scale
        past = past + jnp.concatenate([bias[own]] * HEADS_PER_CHIP, axis=0)
        new = jnp.where(new_live, new, -1e30)
        top = jnp.maximum(
            jnp.max(past, axis=1, keepdims=True), jnp.max(new, axis=1, keepdims=True)
        )
        past = jnp.exp(past - top)
        new = jnp.exp(new - top)
        weight = jnp.sum(past, axis=1, keepdims=True) + jnp.sum(new, axis=1, keepdims=True)
        past = (past / weight).astype(BF16)
        new = (new / weight).astype(BF16)
        mixed = jnp.dot(past, values, preferred_element_type=F32)
        mixed = mixed + jnp.dot(new, new_values[own], preferred_element_type=F32)
        mixed = mixed.astype(BF16)
        for h in range(HEADS_PER_CHIP):
            out[own, HD * h : HD * (h + 1)] = mixed[16 * h : 16 * (h + 1)]


def attend(parts, cosine, sine, bias, cache, layer):
    whole = lambda *shape: pl.BlockSpec(shape, lambda i: (0,) * len(shape))
    return pl.pallas_call(
        attend_kernel,
        grid=(1,),
        in_specs=[
            whole(SECTIONS, 64, SENT),
            whole(64, HD),
            whole(64, HD),
            whole(64, 512),
            pl.BlockSpec((CHIPS, None, 2, 128, HD), lambda i: (0, layer, 0, 0, 0)),
        ],
        out_specs=whole(64, WIDTH),
        out_shape=jax.ShapeDtypeStruct((64, WIDTH), BF16),
        compiler_params=pltpu.CompilerParams(vmem_limit_bytes=32 * 2**20),
        cost_estimate=pl.CostEstimate(
            flops=2**28, bytes_accessed=2 * 2**20, transcendentals=2**17
        ),
        name="attend",
    )(parts, cosine, sine, bias, cache)


def output_kernel(first, second, third, fourth, order, wo_mine, wo_other, out, ordered):
    @pl.when(pl.program_id(0) == 0)
    def _():
        mixed = jnp.concatenate([first[...], second[...], third[...], fourth[...]], axis=0)
        ordered[...] = jnp.dot(order[...], mixed, preferred_element_type=F32).astype(BF16)

    half = WIDTH // 2
    terms = jnp.dot(ordered[:, :half], wo_mine[...], preferred_element_type=F32)
    terms = terms + jnp.dot(ordered[:, half:], wo_other[...], preferred_element_type=F32)
    out[...] = terms.astype(BF16).reshape(out.shape)


def output_terms(gathered, order, wo_mine, wo_other, layer):
    quarter = wo_mine.shape[2]
    chunk = quarter // 4
    return pl.pallas_call(
        output_kernel,
        grid=(quarter // chunk,),
        in_specs=[pl.BlockSpec((64, WIDTH), lambda n: (0, 0))] * SECTIONS
        + [
            pl.BlockSpec((256, 256), lambda n: (0, 0)),
            pl.BlockSpec((None, 256, chunk), lambda n: (layer, 0, n)),
            pl.BlockSpec((None, 256, chunk), lambda n: (layer, 0, n)),
        ],
        out_specs=pl.BlockSpec((CHIPS, 16, chunk), lambda n: (0, 0, n)),
        out_shape=jax.ShapeDtypeStruct((CHIPS, 16, quarter), BF16),
        scratch_shapes=[pltpu.VMEM((256, WIDTH), BF16)],
        compiler_params=pltpu.CompilerParams(vmem_limit_bytes=32 * 2**20),
        cost_estimate=pl.CostEstimate(
            flops=2 * 256 * WIDTH * quarter, bytes_accessed=4 * 2**20, transcendentals=0
        ),
        name="output_terms",
    )(*gathered, order, wo_mine, wo_other)


def body(
    token_ids,
    embedding,
    norm_gain,
    query_weight,
    keyval_weight,
    output_weight,
    prefix_cache,
    prefix_lengths,
):
    section_pos = lax.axis_index("section")
    tensor_pos = lax.axis_index("tensor")
    core, chip = tensor_pos % CORES, tensor_pos // CORES
    quarter = query_weight.shape[1] // SECTIONS

    kv_mine = section_exchange(keyval_weight[0].T.reshape(64, SECTIONS, quarter).transpose(1, 0, 2))
    wq_mine = section_exchange(query_weight[0].reshape(SECTIONS, quarter, 256))
    hidden, gains, lengths = embed(
        token_ids, embedding, prefix_lengths, norm_gain, section_pos, core
    )
    cache = section_exchange(prefix_cache[0])
    wo_mine = section_exchange(output_weight[0].reshape(256, SECTIONS, quarter).transpose(1, 0, 2))
    wq_other = core_swap(wq_mine)
    wo_other = core_swap(wo_mine)

    first = chip_send(kv_mine, lambda p: 2 * p if p < 8 else 2 * (p - 8) + 1)
    second = chip_send(kv_mine, lambda p: 2 * p + 1 if p < 8 else 2 * (p - 8))
    even = chip % 2 == 0
    heads_t = []
    for half in (jnp.where(even, first, second), jnp.where(even, second, first)):
        other = core_swap(half)
        low = jnp.where(core == 0, half, other)
        high = jnp.where(core == 0, other, half)
        heads_t.append(jnp.concatenate([low, high], axis=1))
    keys_t, values_t = heads_t

    cache = cache.reshape(SECTIONS, 128, 2, 8, HD).transpose(3, 0, 2, 1, 4)
    cache = plane_exchange(jnp.repeat(cache, 2, axis=0))

    frequency = ROPE_BASE ** (-(jnp.arange(HD // 2, dtype=F32) * 2.0 / HD))
    positions = (lengths[:, None] + jnp.arange(STEPS)[None, :]).reshape(-1).astype(F32)
    angles = positions[:, None] * frequency[None, :]
    cosine = jnp.concatenate([jnp.cos(angles)] * 2, axis=-1)
    sine = jnp.concatenate([jnp.sin(angles)] * 2, axis=-1)
    row, column = jnp.arange(64)[:, None], jnp.arange(512)[None, :]
    live = jnp.repeat(lengths, STEPS)[:, None]
    live = (row % 16 // 4 == column // 128) & (column % 128 < live)
    bias = jnp.where(live, 0.0, -1e30).astype(F32)
    forward, backward = row_orders(section_pos)

    for layer in range(SECTIONS):
        scaled = (hidden * gains[layer]).astype(BF16)
        rows = plane_exchange(jnp.broadcast_to(scaled[None], (CHIPS, 16, quarter)))
        partial = project(rows, forward, gains, layer, wq_mine, wq_other, keys_t, values_t)
        mixed = attend(section_exchange(partial), cosine, sine, bias, cache, layer)
        gathered = [section_send(mixed, d) for d in range(SECTIONS)]
        terms = plane_exchange(output_terms(gathered, backward, wo_mine, wo_other, layer))
        hidden = hidden + jnp.sum(terms.astype(F32), axis=0)

    finals = section_exchange(hidden.reshape(4, STEPS, quarter).transpose(1, 0, 2))
    return finals.transpose(1, 0, 2).reshape(1, 4, SECTIONS * quarter)


def solution(mesh):
    in_specs = (
        P(),
        P("section", "tensor"),
        P("section", None),
        P("section", None, "tensor"),
        P("section", None, "tensor"),
        P("section", "tensor", None),
        P("section", "tensor", None, None, None),
        P("tensor"),
    )
    out_specs = P("section", "tensor", None)
    return jax.shard_map(body, mesh=mesh, in_specs=in_specs, out_specs=out_specs, check_vma=False)
```

```python
import jax
import jax.numpy as jnp
from jax import lax
from jax.experimental import pallas as pl
from jax.experimental.pallas import tpu as pltpu
from jax.sharding import PartitionSpec as P

HD = 128
NORM_EPSILON = 1e-05
ROPE_BASE = 500000.0
SECTIONS = 4
CHIPS = 16
CORES = 2
STEPS = 4
HEADS_PER_CHIP = 4
BF16 = jnp.bfloat16
F32 = jnp.float32
PLANE = [[2 * p + c for p in range(CHIPS)] for c in range(CORES)]


def section_send(block, distance):
    if distance == 0:
        return block
    route = [(i, (i + distance) % SECTIONS) for i in range(SECTIONS)]
    return lax.ppermute(block, "section", route)


def core_swap(block):
    return lax.ppermute(block, "tensor", [(i, i ^ 1) for i in range(CHIPS * CORES)])


def chip_send(block, target):
    route = [(2 * p + c, 2 * target(p) + c) for p in range(CHIPS) for c in range(CORES)]
    return lax.ppermute(block, "tensor", route)


def plane_exchange(blocks):
    return lax.all_to_all(
        blocks, "tensor", split_axis=0, concat_axis=0, tiled=True, axis_index_groups=PLANE
    )


def section_exchange(blocks):
    return lax.all_to_all(blocks, "section", split_axis=0, concat_axis=0, tiled=True)


def in_three(values):
    high = lax.reduce_precision(values, 8, 7)
    middle = lax.reduce_precision(values - high, 8, 7)
    return [part.astype(BF16) for part in (high, middle, values - high - middle)]


def embed(token_ids, embedding, prefix_lengths, norm_gain, kv_mat, cached, section_pos, core):
    vocab_part, width = embedding.shape
    local_ids = token_ids.T.reshape(-1) - section_pos * vocab_part
    inside = (local_ids >= 0) & (local_ids < vocab_part)
    picked = jnp.take(embedding, jnp.clip(local_ids, 0, vocab_part - 1), axis=0)
    picked = jnp.where(inside[:, None], picked, jnp.zeros_like(picked))
    picked = picked.reshape(CHIPS * CORES, 16, width)
    extra = jnp.pad(prefix_lengths.astype(BF16)[None, :], ((0, 7), (0, width - 4)))
    extra = jnp.broadcast_to(extra[None], (CHIPS * CORES, 8, width))
    by_row = lax.all_to_all(
        jnp.concatenate([picked, extra], axis=1), "tensor", split_axis=0, concat_axis=0, tiled=True
    )
    lengths = by_row[:, 16, :4].reshape(CHIPS, CORES, 4)
    lengths = lax.dynamic_index_in_dim(lengths, core, 1, keepdims=False)
    lengths = lax.dynamic_index_in_dim(lengths, section_pos, 1, keepdims=False)
    gains = jnp.stack(in_three(norm_gain.reshape(CHIPS * CORES, width)), axis=1)
    gains = jnp.pad(gains, ((0, 0), (0, 5), (0, 0)))
    by_row, cached = lax.optimization_barrier((by_row, cached))
    kv_mat = kv_mat.reshape(64, CHIPS * CORES, width).transpose(1, 0, 2)
    by_quarter = section_exchange(jnp.concatenate([by_row[:, :16], gains, kv_mat], axis=1))
    by_quarter = by_quarter.reshape(SECTIONS, 8, 88, width)
    kv_mine = by_quarter[:, :, 24:].transpose(0, 2, 1, 3).reshape(SECTIONS, 64, -1)
    by_quarter = by_quarter[:, :, :24].astype(F32)
    columns = jnp.sum(by_quarter[:, :, :16], axis=0).transpose(1, 0, 2).reshape(16, -1)
    gains = (by_quarter[:, :, 16] + by_quarter[:, :, 17]) + by_quarter[:, :, 18]
    return columns, gains.reshape(SECTIONS, 1, -1), lengths.astype(jnp.int32), kv_mine, cached


def row_orders(section_pos):
    place = jnp.arange(256)[:, None]
    source = jnp.arange(256)[None, :]
    wanted = place // 4 % CHIPS * 16 + place // 64 * 4 + place % 4
    forward = (wanted == source).astype(BF16)
    held = source // 4 % CHIPS * 16 + (section_pos - source // 64) % SECTIONS * 4 + source % 4
    backward = (held == place).astype(BF16)
    return forward, backward


TRANSPOSED = (((1,), (1,)), ((), ()))
WIDTH = HEADS_PER_CHIP * HD
SENT = WIDTH + 3 * HD


def project_kernel(slot, rows, order, gain, *refs):
    wq_mine, wq_other = refs[:SECTIONS], refs[SECTIONS : 2 * SECTIONS]
    keys_t, values_t, out, total = refs[2 * SECTIONS :]
    step = pl.program_id(0)

    @pl.when(step == 0)
    def _():
        total[...] = jnp.zeros_like(total)

    block = rows[...].reshape(256, rows.shape[2])
    block = jnp.dot(order[...], block, preferred_element_type=F32).astype(BF16)
    plain = block.astype(F32) / gain[...]
    half = WIDTH // 2
    for d in range(SECTIONS):

        @pl.when(slot[0] == d)
        def _():
            total[:, :half] += jnp.dot(block, wq_mine[d][...], preferred_element_type=F32)
            total[:, half:WIDTH] += jnp.dot(block, wq_other[d][...], preferred_element_type=F32)

    for start, weight in ((WIDTH, keys_t), (WIDTH + HD, values_t)):
        total[:, start : start + HD] += lax.dot_general(
            block, weight[...], TRANSPOSED, preferred_element_type=F32
        )
    total[:, WIDTH + 2 * HD :] += jnp.sum(plain * plain, axis=1, keepdims=True)

    @pl.when(step == pl.num_programs(0) - 1)
    def _():
        squares = total[:, WIDTH + 2 * HD :]
        high = squares.astype(BF16).astype(F32)
        middle = (squares - high).astype(BF16).astype(F32)
        low = squares - high - middle
        lane = lax.broadcasted_iota(jnp.int32, squares.shape, 1)
        parts = jnp.where(lane == 0, high, jnp.where(lane == 1, middle, low))
        parts = jnp.where(lane < 3, parts, 0.0)
        for j in range(SECTIONS):
            own = slice(64 * j, 64 * (j + 1))
            out[j, :, : WIDTH + 2 * HD] = total[own, : WIDTH + 2 * HD].astype(BF16)
            out[j, :, WIDTH + 2 * HD :] = parts[own].astype(BF16)


def chosen(d, k, slot):
    return jnp.where(slot[0] == d, k, 0)


def project(rows, order, gain, layer, slot, wq_mine, wq_other, keys_t, values_t):
    quarter = rows.shape[2]
    chunk = quarter // 4
    flops = 2 * 256 * quarter * (256 + WIDTH + 2 * HD)
    pieces = [
        pl.BlockSpec((chunk, 256), lambda k, slot, d=d: (chosen(d, k, slot), 0))
        for d in range(SECTIONS)
    ]
    return pl.pallas_call(
        project_kernel,
        grid_spec=pltpu.PrefetchScalarGridSpec(
            num_scalar_prefetch=1,
            grid=(quarter // chunk,),
            in_specs=[
                pl.BlockSpec((CHIPS, 16, chunk), lambda k, slot: (0, 0, k)),
                pl.BlockSpec((256, 256), lambda k, slot: (0, 0)),
                pl.BlockSpec((None, 1, chunk), lambda k, slot: (layer, 0, k)),
                *pieces,
                *pieces,
                pl.BlockSpec((None, HD, chunk), lambda k, slot: (layer, 0, k)),
                pl.BlockSpec((None, HD, chunk), lambda k, slot: (layer, 0, k)),
            ],
            out_specs=pl.BlockSpec((SECTIONS, 64, SENT), lambda k, slot: (0, 0, 0)),
            scratch_shapes=[pltpu.VMEM((256, SENT), F32)],
        ),
        out_shape=jax.ShapeDtypeStruct((SECTIONS, 64, SENT), BF16),
        compiler_params=pltpu.CompilerParams(vmem_limit_bytes=32 * 2**20),
        cost_estimate=pl.CostEstimate(flops=flops, bytes_accessed=5 * 2**20, transcendentals=0),
        name="project",
    )(slot, rows, order, gain, *wq_mine, *wq_other, keys_t, values_t)


def attend_kernel(slot, parts, cosine, sine, bias, cache, out):
    total = parts[0].astype(F32)
    for i in range(1, SECTIONS):
        total = total + parts[i].astype(F32)
    squares = jnp.sum(total[:, WIDTH + 2 * HD :], axis=1, keepdims=True)
    scaling = lax.rsqrt(squares / 8192.0 + NORM_EPSILON)
    turned_cos = cosine[...] * scaling
    turned_sin = sine[...] * scaling

    def turn(vectors):
        half = HD // 2
        swapped = jnp.concatenate([-vectors[:, half:], vectors[:, :half]], axis=1)
        return (vectors * turned_cos + swapped * turned_sin).astype(BF16)

    queries = [turn(total[:, HD * h : HD * (h + 1)]) for h in range(HEADS_PER_CHIP)]
    new_keys = turn(total[:, WIDTH : WIDTH + HD])
    new_values = (total[:, WIDTH + HD : WIDTH + 2 * HD] * scaling).astype(BF16)
    row = lax.broadcasted_iota(jnp.int32, (64, 16), 0) % 16
    column = lax.broadcasted_iota(jnp.int32, (64, 16), 1)
    new_live = (row // 4 == column // 4) & (column % 4 <= row % 4)
    scale = HD**-0.5
    for g in range(4):
        own = slice(16 * g, 16 * (g + 1))
        query = jnp.concatenate([q[own] for q in queries], axis=0)
        keys = cache[4 * g : 4 * (g + 1), 0].reshape(4 * 128, HD)
        values = cache[4 * g : 4 * (g + 1), 1].reshape(4 * 128, HD)
        past = lax.dot_general(query, keys, TRANSPOSED, preferred_element_type=F32) * scale
        new = lax.dot_general(query, new_keys[own], TRANSPOSED, preferred_element_type=F32) * scale
        past = past + jnp.concatenate([bias[own]] * HEADS_PER_CHIP, axis=0)
        new = jnp.where(new_live, new, -1e30)
        top = jnp.maximum(
            jnp.max(past, axis=1, keepdims=True), jnp.max(new, axis=1, keepdims=True)
        )
        past = jnp.exp(past - top)
        new = jnp.exp(new - top)
        weight = jnp.sum(past, axis=1, keepdims=True) + jnp.sum(new, axis=1, keepdims=True)
        past = (past / weight).astype(BF16)
        new = (new / weight).astype(BF16)
        mixed = jnp.dot(past, values, preferred_element_type=F32)
        mixed = mixed + jnp.dot(new, new_values[own], preferred_element_type=F32)
        mixed = mixed.astype(BF16)
        for h in range(HEADS_PER_CHIP):
            out[own, HD * h : HD * (h + 1)] = mixed[16 * h : 16 * (h + 1)]


def attend(parts, cosine, sine, bias, cache, slot):
    whole = lambda *shape: pl.BlockSpec(shape, lambda i, slot: (0,) * len(shape))
    return pl.pallas_call(
        attend_kernel,
        grid_spec=pltpu.PrefetchScalarGridSpec(
            num_scalar_prefetch=1,
            grid=(1,),
            in_specs=[
                whole(SECTIONS, 64, SENT),
                whole(64, HD),
                whole(64, HD),
                whole(64, 512),
                pl.BlockSpec((CHIPS, None, 2, 128, HD), lambda i, slot: (0, slot[0], 0, 0, 0)),
            ],
            out_specs=whole(64, WIDTH),
        ),
        out_shape=jax.ShapeDtypeStruct((64, WIDTH), BF16),
        compiler_params=pltpu.CompilerParams(vmem_limit_bytes=32 * 2**20),
        cost_estimate=pl.CostEstimate(
            flops=2**28, bytes_accessed=2 * 2**20, transcendentals=2**17
        ),
        name="attend",
    )(slot, parts, cosine, sine, bias, cache)


def output_kernel(slot, first, second, third, fourth, order, *refs):
    wo_mine, wo_other = refs[:SECTIONS], refs[SECTIONS : 2 * SECTIONS]
    out, ordered = refs[2 * SECTIONS :]

    @pl.when(pl.program_id(0) == 0)
    def _():
        mixed = jnp.concatenate([first[...], second[...], third[...], fourth[...]], axis=0)
        ordered[...] = jnp.dot(order[...], mixed, preferred_element_type=F32).astype(BF16)

    half = WIDTH // 2
    for d in range(SECTIONS):

        @pl.when(slot[0] == d)
        def _():
            terms = jnp.dot(ordered[:, :half], wo_mine[d][...], preferred_element_type=F32)
            terms = terms + jnp.dot(
                ordered[:, half:], wo_other[d][...], preferred_element_type=F32
            )
            out[...] = terms.astype(BF16).reshape(out.shape)


def output_terms(gathered, order, slot, wo_mine, wo_other):
    quarter = wo_mine[0].shape[1]
    chunk = quarter // 4
    pieces = [
        pl.BlockSpec((256, chunk), lambda n, slot, d=d: (0, chosen(d, n, slot)))
        for d in range(SECTIONS)
    ]
    return pl.pallas_call(
        output_kernel,
        grid_spec=pltpu.PrefetchScalarGridSpec(
            num_scalar_prefetch=1,
            grid=(quarter // chunk,),
            in_specs=[pl.BlockSpec((64, WIDTH), lambda n, slot: (0, 0))] * SECTIONS
            + [pl.BlockSpec((256, 256), lambda n, slot: (0, 0)), *pieces, *pieces],
            out_specs=pl.BlockSpec((CHIPS, 16, chunk), lambda n, slot: (0, 0, n)),
            scratch_shapes=[pltpu.VMEM((256, WIDTH), BF16)],
        ),
        out_shape=jax.ShapeDtypeStruct((CHIPS, 16, quarter), BF16),
        compiler_params=pltpu.CompilerParams(vmem_limit_bytes=32 * 2**20),
        cost_estimate=pl.CostEstimate(
            flops=2 * 256 * WIDTH * quarter, bytes_accessed=4 * 2**20, transcendentals=0
        ),
        name="output_terms",
    )(slot, *gathered, order, *wo_mine, *wo_other)


def body(
    token_ids,
    embedding,
    norm_gain,
    query_weight,
    keyval_weight,
    output_weight,
    prefix_cache,
    prefix_lengths,
):
    section_pos = lax.axis_index("section")
    tensor_pos = lax.axis_index("tensor")
    core, chip = tensor_pos % CORES, tensor_pos // CORES
    quarter = query_weight.shape[1] // SECTIONS

    def share(array, axis, size, distance):
        start = (section_pos + distance) % SECTIONS * size
        return section_send(lax.dynamic_slice_in_dim(array, start, size, axis), distance)

    distances = range(SECTIONS)
    wq_mine = [share(query_weight[0], 0, quarter, d) for d in distances]
    cached = [share(prefix_cache[0], 0, 1, d) for d in distances]
    hidden, gains, lengths, kv_mine, cached = embed(
        token_ids,
        embedding,
        prefix_lengths,
        norm_gain,
        keyval_weight[0].T,
        cached,
        section_pos,
        core,
    )
    cached, wq_mine[1], wq_mine[3] = lax.optimization_barrier((cached, wq_mine[1], wq_mine[3]))
    cached = [c.reshape(1, 128, 2, 8, HD).transpose(3, 0, 2, 1, 4) for c in cached]
    cache = plane_exchange(jnp.repeat(jnp.concatenate(cached, axis=1), 2, axis=0))
    hidden, cache, wq_mine[2] = lax.optimization_barrier((hidden, cache, wq_mine[2]))
    wo_mine = [share(output_weight[0], 1, quarter, d) for d in distances]
    wq_other = [core_swap(w) for w in wq_mine]
    first = chip_send(kv_mine, lambda p: 2 * p if p < 8 else 2 * (p - 8) + 1)
    second = chip_send(kv_mine, lambda p: 2 * p + 1 if p < 8 else 2 * (p - 8))
    even = chip % 2 == 0
    heads_t = []
    for half in (jnp.where(even, first, second), jnp.where(even, second, first)):
        other = core_swap(half)
        low = jnp.where(core == 0, half, other)
        high = jnp.where(core == 0, other, half)
        heads_t.append(jnp.concatenate([low, high], axis=1))
    keys_t, values_t = heads_t

    def gather_rows(layer):
        scaled = (hidden * gains[layer]).astype(BF16)
        return plane_exchange(jnp.broadcast_to(scaled[None], (CHIPS, 16, quarter)))

    rows = gather_rows(0)
    rows, wo_mine[1], wo_mine[3] = lax.optimization_barrier((rows, wo_mine[1], wo_mine[3]))
    frequency = ROPE_BASE ** (-(jnp.arange(HD // 2, dtype=F32) * 2.0 / HD))
    positions = (lengths[:, None] + jnp.arange(STEPS)[None, :]).reshape(-1).astype(F32)
    angles = positions[:, None] * frequency[None, :]
    cosine = jnp.concatenate([jnp.cos(angles)] * 2, axis=-1)
    sine = jnp.concatenate([jnp.sin(angles)] * 2, axis=-1)
    row, column = jnp.arange(64)[:, None], jnp.arange(512)[None, :]
    live = jnp.repeat(lengths, STEPS)[:, None]
    live = (row % 16 // 4 == column // 128) & (column % 128 < live)
    bias = jnp.where(live, 0.0, -1e30).astype(F32)
    forward, backward = row_orders(section_pos)

    for layer in range(SECTIONS):
        slot = ((section_pos - layer) % SECTIONS).reshape(1)
        if layer > 0:
            rows = gather_rows(layer)
        partial = project(rows, forward, gains, layer, slot, wq_mine, wq_other, keys_t, values_t)
        parts = section_exchange(partial)
        if layer == 0:
            parts, wo_mine = lax.optimization_barrier((parts, wo_mine))
            wo_other = [core_swap(w) for w in wo_mine]
        mixed = attend(parts, cosine, sine, bias, cache, slot)
        gathered = [section_send(mixed, d) for d in distances]
        terms = plane_exchange(output_terms(gathered, backward, slot, wo_mine, wo_other))
        hidden = hidden + jnp.sum(terms.astype(F32), axis=0)

    finals = section_exchange(hidden.reshape(4, STEPS, quarter).transpose(1, 0, 2))
    return finals.transpose(1, 0, 2).reshape(1, 4, SECTIONS * quarter)


def solution(mesh):
    in_specs = (
        P(),
        P("section", "tensor"),
        P("section", None),
        P("section", None, "tensor"),
        P("section", None, "tensor"),
        P("section", "tensor", None),
        P("section", "tensor", None, None, None),
        P("tensor"),
    )
    out_specs = P("section", "tensor", None)
    return jax.shard_map(body, mesh=mesh, in_specs=in_specs, out_specs=out_specs, check_vma=False)
```

```python
import jax
import jax.numpy as jnp
from jax import lax
from jax.experimental import pallas as pl
from jax.experimental.pallas import tpu as pltpu
from jax.sharding import PartitionSpec as P

HD = 128
NORM_EPSILON = 1e-05
ROPE_BASE = 500000.0
SECTIONS = 4
CHIPS = 16
CORES = 2
STEPS = 4
HEADS_PER_CHIP = 4
BF16 = jnp.bfloat16
F32 = jnp.float32
PLANE = [[2 * p + c for p in range(CHIPS)] for c in range(CORES)]


def section_send(block, distance):
    if distance == 0:
        return block
    route = [(i, (i + distance) % SECTIONS) for i in range(SECTIONS)]
    return lax.ppermute(block, "section", route)


def core_swap(block):
    return lax.ppermute(block, "tensor", [(i, i ^ 1) for i in range(CHIPS * CORES)])


def chip_send(block, target):
    route = [(2 * p + c, 2 * target(p) + c) for p in range(CHIPS) for c in range(CORES)]
    return lax.ppermute(block, "tensor", route)


def plane_exchange(blocks):
    return lax.all_to_all(
        blocks, "tensor", split_axis=0, concat_axis=0, tiled=True, axis_index_groups=PLANE
    )


def section_exchange(blocks):
    return lax.all_to_all(blocks, "section", split_axis=0, concat_axis=0, tiled=True)


def in_three(values):
    high = lax.reduce_precision(values, 8, 7)
    middle = lax.reduce_precision(values - high, 8, 7)
    return [part.astype(BF16) for part in (high, middle, values - high - middle)]


def embed(token_ids, embedding, prefix_lengths, norm_gain, early, section_pos, core):
    vocab_part, width = embedding.shape
    local_ids = token_ids.T.reshape(-1) - section_pos * vocab_part
    inside = (local_ids >= 0) & (local_ids < vocab_part)
    picked = jnp.take(embedding, jnp.clip(local_ids, 0, vocab_part - 1), axis=0)
    picked = jnp.where(inside[:, None], picked, jnp.zeros_like(picked))
    picked = picked.reshape(CHIPS * CORES, 16, width)
    extra = jnp.pad(prefix_lengths.astype(BF16)[None, :], ((0, 7), (0, width - 4)))
    extra = jnp.broadcast_to(extra[None], (CHIPS * CORES, 8, width))
    picked = jnp.concatenate([picked, extra], axis=1)
    kv_mine, cached = early
    picked, kv_mine = lax.optimization_barrier((picked, kv_mine))
    by_row = lax.all_to_all(picked, "tensor", split_axis=0, concat_axis=0, tiled=True)
    by_row, cached = lax.optimization_barrier((by_row, cached))
    lengths = by_row[:, 16, :4].reshape(CHIPS, CORES, 4)
    lengths = lax.dynamic_index_in_dim(lengths, core, 1, keepdims=False)
    lengths = lax.dynamic_index_in_dim(lengths, section_pos, 1, keepdims=False)
    gains = jnp.stack(in_three(norm_gain.reshape(CHIPS * CORES, width)), axis=1)
    gains = jnp.pad(gains, ((0, 0), (0, 5), (0, 0)))
    by_quarter = section_exchange(jnp.concatenate([by_row[:, :16], gains], axis=1))
    by_quarter = by_quarter.reshape(SECTIONS, 8, 24, width).astype(F32)
    columns = jnp.sum(by_quarter[:, :, :16], axis=0).transpose(1, 0, 2).reshape(16, -1)
    gains = (by_quarter[:, :, 16] + by_quarter[:, :, 17]) + by_quarter[:, :, 18]
    return columns, gains.reshape(SECTIONS, 1, -1), lengths.astype(jnp.int32), (kv_mine, cached)


def row_orders(section_pos):
    place = jnp.arange(256)[:, None]
    source = jnp.arange(256)[None, :]
    wanted = place // 4 % CHIPS * 16 + place // 64 * 4 + place % 4
    forward = (wanted == source).astype(BF16)
    held = source // 4 % CHIPS * 16 + (section_pos - source // 64) % SECTIONS * 4 + source % 4
    backward = (held == place).astype(BF16)
    return forward, backward


TRANSPOSED = (((1,), (1,)), ((), ()))
WIDTH = HEADS_PER_CHIP * HD
SENT = WIDTH + 3 * HD


def by_head_kernel(first, second, third, fourth, out):
    for d, piece in enumerate((first, second, third, fourth)):
        for p in range(CHIPS):
            for i in range(2):
                start = 1024 * i + HD * (p // 2)
                out[p, d, i] = piece[:, start : start + HD]


def by_head(pieces):
    whole = pl.BlockSpec(pieces[0].shape, lambda i: (0, 0))
    shape = (CHIPS, SECTIONS, 2, 128, HD)
    return pl.pallas_call(
        by_head_kernel,
        grid=(1,),
        in_specs=[whole] * SECTIONS,
        out_specs=pl.BlockSpec(shape, lambda i: (0, 0, 0, 0, 0)),
        out_shape=jax.ShapeDtypeStruct(shape, BF16),
        compiler_params=pltpu.CompilerParams(vmem_limit_bytes=32 * 2**20),
        cost_estimate=pl.CostEstimate(flops=0, bytes_accessed=7 * 2**20, transcendentals=0),
        name="by_head",
    )(*pieces)


def project_kernel(slot, rows, order, gain, wq_mine, wq_other, keys_t, values_t, out, total):
    step = pl.program_id(0)

    @pl.when(step == 0)
    def _():
        total[...] = jnp.zeros_like(total)

    block = rows[...].reshape(256, rows.shape[2])
    block = jnp.dot(order[...], block, preferred_element_type=F32).astype(BF16)
    plain = block.astype(F32) / gain[...]
    half = WIDTH // 2
    total[:, :half] += jnp.dot(block, wq_mine[...], preferred_element_type=F32)
    total[:, half:WIDTH] += jnp.dot(block, wq_other[...], preferred_element_type=F32)
    for start, weight in ((WIDTH, keys_t), (WIDTH + HD, values_t)):
        total[:, start : start + HD] += lax.dot_general(
            block, weight[...], TRANSPOSED, preferred_element_type=F32
        )
    total[:, WIDTH + 2 * HD :] += jnp.sum(plain * plain, axis=1, keepdims=True)

    @pl.when(step == pl.num_programs(0) - 1)
    def _():
        squares = total[:, WIDTH + 2 * HD :]
        high = squares.astype(BF16).astype(F32)
        middle = (squares - high).astype(BF16).astype(F32)
        low = squares - high - middle
        lane = lax.broadcasted_iota(jnp.int32, squares.shape, 1)
        parts = jnp.where(lane == 0, high, jnp.where(lane == 1, middle, low))
        parts = jnp.where(lane < 3, parts, 0.0)
        for j in range(SECTIONS):
            own = slice(64 * j, 64 * (j + 1))
            out[j, :, : WIDTH + 2 * HD] = total[own, : WIDTH + 2 * HD].astype(BF16)
            out[j, :, WIDTH + 2 * HD :] = parts[own].astype(BF16)


def project(rows, order, gain, layer, slot, wq_mine, wq_other, keys_t, values_t):
    quarter = rows.shape[2]
    chunk = quarter // 4
    flops = 2 * 256 * quarter * (256 + WIDTH + 2 * HD)
    return pl.pallas_call(
        project_kernel,
        grid_spec=pltpu.PrefetchScalarGridSpec(
            num_scalar_prefetch=1,
            grid=(quarter // chunk,),
            in_specs=[
                pl.BlockSpec((CHIPS, 16, chunk), lambda k, slot: (0, 0, k)),
                pl.BlockSpec((256, 256), lambda k, slot: (0, 0)),
                pl.BlockSpec((None, 1, chunk), lambda k, slot: (layer, 0, k)),
                pl.BlockSpec((chunk, 256), lambda k, slot: (k, 0)),
                pl.BlockSpec((chunk, 256), lambda k, slot: (k, 0)),
                pl.BlockSpec((HD, chunk), lambda k, slot: (0, k)),
                pl.BlockSpec((HD, chunk), lambda k, slot: (0, k)),
            ],
            out_specs=pl.BlockSpec((SECTIONS, 64, SENT), lambda k, slot: (0, 0, 0)),
            scratch_shapes=[pltpu.VMEM((256, SENT), F32)],
        ),
        out_shape=jax.ShapeDtypeStruct((SECTIONS, 64, SENT), BF16),
        compiler_params=pltpu.CompilerParams(vmem_limit_bytes=24 * 2**20),
        cost_estimate=pl.CostEstimate(flops=flops, bytes_accessed=5 * 2**20, transcendentals=0),
        name="project",
    )(slot, rows, order, gain, wq_mine, wq_other, keys_t, values_t)


def attend_kernel(slot, parts, cosine, sine, bias, cache, out):
    total = parts[0].astype(F32)
    for i in range(1, SECTIONS):
        total = total + parts[i].astype(F32)
    squares = jnp.sum(total[:, WIDTH + 2 * HD :], axis=1, keepdims=True)
    scaling = lax.rsqrt(squares / 8192.0 + NORM_EPSILON)
    turned_cos = cosine[...] * scaling
    turned_sin = sine[...] * scaling

    def turn(vectors):
        half = HD // 2
        swapped = jnp.concatenate([-vectors[:, half:], vectors[:, :half]], axis=1)
        return (vectors * turned_cos + swapped * turned_sin).astype(BF16)

    queries = [turn(total[:, HD * h : HD * (h + 1)]) for h in range(HEADS_PER_CHIP)]
    new_keys = turn(total[:, WIDTH : WIDTH + HD])
    new_values = (total[:, WIDTH + HD : WIDTH + 2 * HD] * scaling).astype(BF16)
    row = lax.broadcasted_iota(jnp.int32, (64, 16), 0) % 16
    column = lax.broadcasted_iota(jnp.int32, (64, 16), 1)
    new_live = (row // 4 == column // 4) & (column % 4 <= row % 4)
    scale = HD**-0.5
    for g in range(4):
        own = slice(16 * g, 16 * (g + 1))
        query = jnp.concatenate([q[own] for q in queries], axis=0)
        keys = cache[4 * g : 4 * (g + 1), 0].reshape(4 * 128, HD)
        values = cache[4 * g : 4 * (g + 1), 1].reshape(4 * 128, HD)
        past = lax.dot_general(query, keys, TRANSPOSED, preferred_element_type=F32) * scale
        new = lax.dot_general(query, new_keys[own], TRANSPOSED, preferred_element_type=F32) * scale
        past = past + jnp.concatenate([bias[own]] * HEADS_PER_CHIP, axis=0)
        new = jnp.where(new_live, new, -1e30)
        top = jnp.maximum(
            jnp.max(past, axis=1, keepdims=True), jnp.max(new, axis=1, keepdims=True)
        )
        past = jnp.exp(past - top)
        new = jnp.exp(new - top)
        weight = jnp.sum(past, axis=1, keepdims=True) + jnp.sum(new, axis=1, keepdims=True)
        past = (past / weight).astype(BF16)
        new = (new / weight).astype(BF16)
        mixed = jnp.dot(past, values, preferred_element_type=F32)
        mixed = mixed + jnp.dot(new, new_values[own], preferred_element_type=F32)
        mixed = mixed.astype(BF16)
        for h in range(HEADS_PER_CHIP):
            out[own, HD * h : HD * (h + 1)] = mixed[16 * h : 16 * (h + 1)]


def attend(parts, cosine, sine, bias, cache, slot):
    whole = lambda *shape: pl.BlockSpec(shape, lambda i, slot: (0,) * len(shape))
    return pl.pallas_call(
        attend_kernel,
        grid_spec=pltpu.PrefetchScalarGridSpec(
            num_scalar_prefetch=1,
            grid=(1,),
            in_specs=[
                whole(SECTIONS, 64, SENT),
                whole(64, HD),
                whole(64, HD),
                whole(64, 512),
                pl.BlockSpec((CHIPS, None, 2, 128, HD), lambda i, slot: (0, slot[0], 0, 0, 0)),
            ],
            out_specs=whole(64, WIDTH),
        ),
        out_shape=jax.ShapeDtypeStruct((64, WIDTH), BF16),
        compiler_params=pltpu.CompilerParams(vmem_limit_bytes=32 * 2**20),
        cost_estimate=pl.CostEstimate(
            flops=2**28, bytes_accessed=2 * 2**20, transcendentals=2**17
        ),
        name="attend",
    )(slot, parts, cosine, sine, bias, cache)


def output_kernel(slot, first, second, third, fourth, order, wo_mine, wo_other, out, ordered):
    @pl.when(pl.program_id(0) == 0)
    def _():
        mixed = jnp.concatenate([first[...], second[...], third[...], fourth[...]], axis=0)
        ordered[...] = jnp.dot(order[...], mixed, preferred_element_type=F32).astype(BF16)

    half = WIDTH // 2
    terms = jnp.dot(ordered[:, :half], wo_mine[...], preferred_element_type=F32)
    terms = terms + jnp.dot(ordered[:, half:], wo_other[...], preferred_element_type=F32)
    out[...] = terms.astype(BF16).reshape(out.shape)


def output_terms(gathered, order, slot, wo_mine, wo_other):
    quarter = wo_mine.shape[1]
    chunk = quarter // 4
    return pl.pallas_call(
        output_kernel,
        grid_spec=pltpu.PrefetchScalarGridSpec(
            num_scalar_prefetch=1,
            grid=(quarter // chunk,),
            in_specs=[pl.BlockSpec((64, WIDTH), lambda n, slot: (0, 0))] * SECTIONS
            + [
                pl.BlockSpec((256, 256), lambda n, slot: (0, 0)),
                pl.BlockSpec((256, chunk), lambda n, slot: (0, n)),
                pl.BlockSpec((256, chunk), lambda n, slot: (0, n)),
            ],
            out_specs=pl.BlockSpec((CHIPS, 16, chunk), lambda n, slot: (0, 0, n)),
            scratch_shapes=[pltpu.VMEM((256, WIDTH), BF16)],
        ),
        out_shape=jax.ShapeDtypeStruct((CHIPS, 16, quarter), BF16),
        compiler_params=pltpu.CompilerParams(vmem_limit_bytes=24 * 2**20),
        cost_estimate=pl.CostEstimate(
            flops=2 * 256 * WIDTH * quarter, bytes_accessed=4 * 2**20, transcendentals=0
        ),
        name="output_terms",
    )(slot, *gathered, order, wo_mine, wo_other)


def body(
    token_ids,
    embedding,
    norm_gain,
    query_weight,
    keyval_weight,
    output_weight,
    prefix_cache,
    prefix_lengths,
):
    section_pos = lax.axis_index("section")
    tensor_pos = lax.axis_index("tensor")
    core, chip = tensor_pos % CORES, tensor_pos // CORES
    quarter = query_weight.shape[1] // SECTIONS

    def own(array, axis, size, distance):
        start = (section_pos + distance) % SECTIONS * size
        return lax.dynamic_slice_in_dim(array, start, size, axis)

    def share(array, axis, size, distance):
        return section_send(own(array, axis, size, distance), distance)

    distances = range(SECTIONS)
    kv_mine = [share(keyval_weight[0].T, 1, quarter, d) for d in distances]
    rows_first = prefix_cache[0].reshape(SECTIONS, 128, -1)
    cached = [section_send(own(rows_first, 0, 1, d)[0], d) for d in distances]
    hidden, gains, lengths, (kv_mine, cached) = embed(
        token_ids,
        embedding,
        prefix_lengths,
        norm_gain,
        (kv_mine, cached),
        section_pos,
        core,
    )
    kv_mine = jnp.stack(kv_mine)
    first = chip_send(kv_mine, lambda p: 2 * p if p < 8 else 2 * (p - 8) + 1)
    second = chip_send(kv_mine, lambda p: 2 * p + 1 if p < 8 else 2 * (p - 8))
    hidden, query_mat = lax.optimization_barrier((hidden, query_weight[0]))
    wq_mine = [share(query_mat, 0, quarter, d) if d != 2 else None for d in distances]

    def gather_rows(layer):
        scaled = (hidden * gains[layer]).astype(BF16)
        return plane_exchange(jnp.broadcast_to(scaled[None], (CHIPS, 16, quarter)))

    rows = gather_rows(0)
    rows, cached, first, second, wq_mine[1], wq_mine[3], query_mat = lax.optimization_barrier(
        (rows, cached, first, second, wq_mine[1], wq_mine[3], query_mat)
    )
    wq_mine[2] = share(query_mat, 0, quarter, 2)
    cache = plane_exchange(by_head(cached))
    wq_mine, output_mat = lax.optimization_barrier((wq_mine, output_weight[0]))
    wo_mine = [share(output_mat, 1, quarter, d) for d in distances]
    wq_other = jnp.stack([core_swap(w) for w in wq_mine])
    wq_mine = jnp.stack(wq_mine)
    wq_mine, wq_other = lax.optimization_barrier((wq_mine, wq_other))
    even = chip % 2 == 0
    heads_t = []
    for half in (jnp.where(even, first, second), jnp.where(even, second, first)):
        other = core_swap(half)
        low = jnp.where(core == 0, half, other)
        high = jnp.where(core == 0, other, half)
        heads_t.append(jnp.concatenate([low, high], axis=1))
    keys_t, values_t = heads_t

    frequency = ROPE_BASE ** (-(jnp.arange(HD // 2, dtype=F32) * 2.0 / HD))
    positions = (lengths[:, None] + jnp.arange(STEPS)[None, :]).reshape(-1).astype(F32)
    angles = positions[:, None] * frequency[None, :]
    cosine = jnp.concatenate([jnp.cos(angles)] * 2, axis=-1)
    sine = jnp.concatenate([jnp.sin(angles)] * 2, axis=-1)
    row, column = jnp.arange(64)[:, None], jnp.arange(512)[None, :]
    live = jnp.repeat(lengths, STEPS)[:, None]
    live = (row % 16 // 4 == column // 128) & (column % 128 < live)
    bias = jnp.where(live, 0.0, -1e30).astype(F32)
    forward, backward = row_orders(section_pos)

    for layer in range(SECTIONS):
        slot = ((section_pos - layer) % SECTIONS).reshape(1)
        pick = lambda held: lax.dynamic_index_in_dim(held, slot[0], 0, keepdims=False)
        if layer > 0:
            rows = gather_rows(layer)
        weights = [pick(w) for w in (wq_mine, wq_other, keys_t, values_t)]
        partial = project(rows, forward, gains, layer, slot, *weights)
        if layer == 0:
            partial, cache = lax.optimization_barrier((partial, cache))
        parts = section_exchange(partial)
        if layer == 0:
            parts, wo_mine = lax.optimization_barrier((parts, wo_mine))
            wo_other = jnp.stack([core_swap(w) for w in wo_mine])
            wo_mine = jnp.stack(wo_mine)
        mixed = attend(parts, cosine, sine, bias, cache, slot)
        gathered = [section_send(mixed, d) for d in distances]
        terms = plane_exchange(
            output_terms(gathered, backward, slot, pick(wo_mine), pick(wo_other))
        )
        hidden = hidden + jnp.sum(terms.astype(F32), axis=0)

    finals = section_exchange(hidden.reshape(4, STEPS, quarter).transpose(1, 0, 2))
    return finals.transpose(1, 0, 2).reshape(1, 4, SECTIONS * quarter)


def solution(mesh):
    in_specs = (
        P(),
        P("section", "tensor"),
        P("section", None),
        P("section", None, "tensor"),
        P("section", None, "tensor"),
        P("section", "tensor", None),
        P("section", "tensor", None, None, None),
        P("tensor"),
    )
    out_specs = P("section", "tensor", None)
    return jax.shard_map(body, mesh=mesh, in_specs=in_specs, out_specs=out_specs, check_vma=False)
```

```python
import jax
import jax.numpy as jnp
from jax import lax
from jax.experimental import pallas as pl
from jax.experimental.pallas import tpu as pltpu
from jax.sharding import PartitionSpec as P

HD = 128
NORM_EPSILON = 1e-05
ROPE_BASE = 500000.0
SECTIONS = 4
CHIPS = 16
CORES = 2
STEPS = 4
HEADS_PER_CHIP = 4
BF16 = jnp.bfloat16
F32 = jnp.float32
PLANE = [[2 * p + c for p in range(CHIPS)] for c in range(CORES)]


def section_send(block, distance):
    if distance == 0:
        return block
    route = [(i, (i + distance) % SECTIONS) for i in range(SECTIONS)]
    return lax.ppermute(block, "section", route)


def core_swap(block):
    return lax.ppermute(block, "tensor", [(i, i ^ 1) for i in range(CHIPS * CORES)])


def chip_send(block, target):
    route = [(2 * p + c, 2 * target(p) + c) for p in range(CHIPS) for c in range(CORES)]
    return lax.ppermute(block, "tensor", route)


def plane_exchange(blocks):
    return lax.all_to_all(
        blocks, "tensor", split_axis=0, concat_axis=0, tiled=True, axis_index_groups=PLANE
    )


def section_exchange(blocks):
    return lax.all_to_all(blocks, "section", split_axis=0, concat_axis=0, tiled=True)


def in_three(values):
    high = lax.reduce_precision(values, 8, 7)
    middle = lax.reduce_precision(values - high, 8, 7)
    return [part.astype(BF16) for part in (high, middle, values - high - middle)]


def embed(token_ids, embedding, prefix_lengths, norm_gain, early, section_pos, core):
    vocab_part, width = embedding.shape
    local_ids = token_ids.T.reshape(-1) - section_pos * vocab_part
    inside = (local_ids >= 0) & (local_ids < vocab_part)
    picked = jnp.take(embedding, jnp.clip(local_ids, 0, vocab_part - 1), axis=0)
    picked = jnp.where(inside[:, None], picked, jnp.zeros_like(picked))
    picked = picked.reshape(CHIPS * CORES, 16, width)
    extra = jnp.pad(prefix_lengths.astype(BF16)[None, :], ((0, 7), (0, width - 4)))
    extra = jnp.broadcast_to(extra[None], (CHIPS * CORES, 8, width))
    picked = jnp.concatenate([picked, extra], axis=1)
    kv_mine, wq_mine = early
    picked, kv_mine = lax.optimization_barrier((picked, kv_mine))
    by_row = lax.all_to_all(picked, "tensor", split_axis=0, concat_axis=0, tiled=True)
    by_row, wq_mine = lax.optimization_barrier((by_row, wq_mine))
    lengths = by_row[:, 16, :4].reshape(CHIPS, CORES, 4)
    lengths = lax.dynamic_index_in_dim(lengths, core, 1, keepdims=False)
    lengths = lax.dynamic_index_in_dim(lengths, section_pos, 1, keepdims=False)
    gains = jnp.stack(in_three(norm_gain.reshape(CHIPS * CORES, width)), axis=1)
    gains = jnp.pad(gains, ((0, 0), (0, 5), (0, 0)))
    by_quarter = section_exchange(jnp.concatenate([by_row[:, :16], gains], axis=1))
    by_quarter = by_quarter.reshape(SECTIONS, 8, 24, width).astype(F32)
    columns = jnp.sum(by_quarter[:, :, :16], axis=0).transpose(1, 0, 2).reshape(16, -1)
    gains = (by_quarter[:, :, 16] + by_quarter[:, :, 17]) + by_quarter[:, :, 18]
    return columns, gains.reshape(SECTIONS, 1, -1), lengths.astype(jnp.int32), (kv_mine, wq_mine)


def row_orders(section_pos):
    place = jnp.arange(256)[:, None]
    source = jnp.arange(256)[None, :]
    wanted = place // 4 % CHIPS * 16 + place // 64 * 4 + place % 4
    forward = (wanted == source).astype(BF16)
    held = source // 4 % CHIPS * 16 + (section_pos - source // 64) % SECTIONS * 4 + source % 4
    backward = (held == place).astype(BF16)
    return forward, backward


TRANSPOSED = (((1,), (1,)), ((), ()))
WIDTH = HEADS_PER_CHIP * HD
SENT = WIDTH + 3 * HD


def by_head_kernel(first, second, third, fourth, out):
    for d, piece in enumerate((first, second, third, fourth)):
        for p in range(CHIPS):
            for i in range(2):
                start = 1024 * i + HD * (p // 2)
                out[p, d, i] = piece[:, start : start + HD]


def by_head(pieces):
    whole = pl.BlockSpec(pieces[0].shape, lambda i: (0, 0))
    shape = (CHIPS, SECTIONS, 2, 128, HD)
    return pl.pallas_call(
        by_head_kernel,
        grid=(1,),
        in_specs=[whole] * SECTIONS,
        out_specs=pl.BlockSpec(shape, lambda i: (0, 0, 0, 0, 0)),
        out_shape=jax.ShapeDtypeStruct(shape, BF16),
        compiler_params=pltpu.CompilerParams(vmem_limit_bytes=32 * 2**20),
        cost_estimate=pl.CostEstimate(flops=0, bytes_accessed=7 * 2**20, transcendentals=0),
        name="by_head",
    )(*pieces)


def project_kernel(slot, rows, order, gain, wq_mine, wq_other, keys_t, values_t, out, total):
    step = pl.program_id(0)

    @pl.when(step == 0)
    def _():
        total[...] = jnp.zeros_like(total)

    block = rows[...].reshape(256, rows.shape[2])
    block = jnp.dot(order[...], block, preferred_element_type=F32).astype(BF16)
    plain = block.astype(F32) / gain[...]
    half = WIDTH // 2
    total[:, :half] += jnp.dot(block, wq_mine[...], preferred_element_type=F32)
    total[:, half:WIDTH] += jnp.dot(block, wq_other[...], preferred_element_type=F32)
    for start, weight in ((WIDTH, keys_t), (WIDTH + HD, values_t)):
        total[:, start : start + HD] += lax.dot_general(
            block, weight[...], TRANSPOSED, preferred_element_type=F32
        )
    total[:, WIDTH + 2 * HD :] += jnp.sum(plain * plain, axis=1, keepdims=True)

    @pl.when(step == pl.num_programs(0) - 1)
    def _():
        squares = total[:, WIDTH + 2 * HD :]
        high = squares.astype(BF16).astype(F32)
        middle = (squares - high).astype(BF16).astype(F32)
        low = squares - high - middle
        lane = lax.broadcasted_iota(jnp.int32, squares.shape, 1)
        parts = jnp.where(lane == 0, high, jnp.where(lane == 1, middle, low))
        parts = jnp.where(lane < 3, parts, 0.0)
        for j in range(SECTIONS):
            own = slice(64 * j, 64 * (j + 1))
            out[j, :, : WIDTH + 2 * HD] = total[own, : WIDTH + 2 * HD].astype(BF16)
            out[j, :, WIDTH + 2 * HD :] = parts[own].astype(BF16)


def project(rows, order, gain, layer, slot, wq_mine, wq_other, keys_t, values_t):
    quarter = rows.shape[2]
    chunk = quarter // 4
    flops = 2 * 256 * quarter * (256 + WIDTH + 2 * HD)
    return pl.pallas_call(
        project_kernel,
        grid_spec=pltpu.PrefetchScalarGridSpec(
            num_scalar_prefetch=1,
            grid=(quarter // chunk,),
            in_specs=[
                pl.BlockSpec((CHIPS, 16, chunk), lambda k, slot: (0, 0, k)),
                pl.BlockSpec((256, 256), lambda k, slot: (0, 0)),
                pl.BlockSpec((None, 1, chunk), lambda k, slot: (layer, 0, k)),
                pl.BlockSpec((chunk, 256), lambda k, slot: (k, 0)),
                pl.BlockSpec((chunk, 256), lambda k, slot: (k, 0)),
                pl.BlockSpec((HD, chunk), lambda k, slot: (0, k)),
                pl.BlockSpec((HD, chunk), lambda k, slot: (0, k)),
            ],
            out_specs=pl.BlockSpec((SECTIONS, 64, SENT), lambda k, slot: (0, 0, 0)),
            scratch_shapes=[pltpu.VMEM((256, SENT), F32)],
        ),
        out_shape=jax.ShapeDtypeStruct((SECTIONS, 64, SENT), BF16),
        compiler_params=pltpu.CompilerParams(vmem_limit_bytes=24 * 2**20),
        cost_estimate=pl.CostEstimate(flops=flops, bytes_accessed=5 * 2**20, transcendentals=0),
        name="project",
    )(slot, rows, order, gain, wq_mine, wq_other, keys_t, values_t)


def attend_kernel(slot, parts, cosine, sine, bias, cache, out):
    total = parts[0].astype(F32)
    for i in range(1, SECTIONS):
        total = total + parts[i].astype(F32)
    squares = jnp.sum(total[:, WIDTH + 2 * HD :], axis=1, keepdims=True)
    scaling = lax.rsqrt(squares / 8192.0 + NORM_EPSILON)
    turned_cos = cosine[...] * scaling
    turned_sin = sine[...] * scaling

    def turn(vectors):
        half = HD // 2
        swapped = jnp.concatenate([-vectors[:, half:], vectors[:, :half]], axis=1)
        return (vectors * turned_cos + swapped * turned_sin).astype(BF16)

    queries = [turn(total[:, HD * h : HD * (h + 1)]) for h in range(HEADS_PER_CHIP)]
    new_keys = turn(total[:, WIDTH : WIDTH + HD])
    new_values = (total[:, WIDTH + HD : WIDTH + 2 * HD] * scaling).astype(BF16)
    row = lax.broadcasted_iota(jnp.int32, (64, 16), 0) % 16
    column = lax.broadcasted_iota(jnp.int32, (64, 16), 1)
    new_live = (row // 4 == column // 4) & (column % 4 <= row % 4)
    scale = HD**-0.5
    for g in range(4):
        own = slice(16 * g, 16 * (g + 1))
        query = jnp.concatenate([q[own] for q in queries], axis=0)
        keys = cache[4 * g : 4 * (g + 1), 0].reshape(4 * 128, HD)
        values = cache[4 * g : 4 * (g + 1), 1].reshape(4 * 128, HD)
        past = lax.dot_general(query, keys, TRANSPOSED, preferred_element_type=F32) * scale
        new = lax.dot_general(query, new_keys[own], TRANSPOSED, preferred_element_type=F32) * scale
        past = past + jnp.concatenate([bias[own]] * HEADS_PER_CHIP, axis=0)
        new = jnp.where(new_live, new, -1e30)
        top = jnp.maximum(
            jnp.max(past, axis=1, keepdims=True), jnp.max(new, axis=1, keepdims=True)
        )
        past = jnp.exp(past - top)
        new = jnp.exp(new - top)
        weight = jnp.sum(past, axis=1, keepdims=True) + jnp.sum(new, axis=1, keepdims=True)
        past = (past / weight).astype(BF16)
        new = (new / weight).astype(BF16)
        mixed = jnp.dot(past, values, preferred_element_type=F32)
        mixed = mixed + jnp.dot(new, new_values[own], preferred_element_type=F32)
        mixed = mixed.astype(BF16)
        for h in range(HEADS_PER_CHIP):
            out[own, HD * h : HD * (h + 1)] = mixed[16 * h : 16 * (h + 1)]


def attend(parts, cosine, sine, bias, cache, slot):
    whole = lambda *shape: pl.BlockSpec(shape, lambda i, slot: (0,) * len(shape))
    return pl.pallas_call(
        attend_kernel,
        grid_spec=pltpu.PrefetchScalarGridSpec(
            num_scalar_prefetch=1,
            grid=(1,),
            in_specs=[
                whole(SECTIONS, 64, SENT),
                whole(64, HD),
                whole(64, HD),
                whole(64, 512),
                pl.BlockSpec((CHIPS, None, 2, 128, HD), lambda i, slot: (0, slot[0], 0, 0, 0)),
            ],
            out_specs=whole(64, WIDTH),
        ),
        out_shape=jax.ShapeDtypeStruct((64, WIDTH), BF16),
        compiler_params=pltpu.CompilerParams(vmem_limit_bytes=32 * 2**20),
        cost_estimate=pl.CostEstimate(
            flops=2**28, bytes_accessed=2 * 2**20, transcendentals=2**17
        ),
        name="attend",
    )(slot, parts, cosine, sine, bias, cache)


def output_kernel(slot, first, second, third, fourth, order, wo_mine, wo_other, out, ordered):
    @pl.when(pl.program_id(0) == 0)
    def _():
        mixed = jnp.concatenate([first[...], second[...], third[...], fourth[...]], axis=0)
        ordered[...] = jnp.dot(order[...], mixed, preferred_element_type=F32).astype(BF16)

    half = WIDTH // 2
    terms = jnp.dot(ordered[:, :half], wo_mine[...], preferred_element_type=F32)
    terms = terms + jnp.dot(ordered[:, half:], wo_other[...], preferred_element_type=F32)
    out[...] = terms.astype(BF16).reshape(out.shape)


def output_terms(gathered, order, slot, wo_mine, wo_other):
    quarter = wo_mine.shape[1]
    chunk = quarter // 4
    return pl.pallas_call(
        output_kernel,
        grid_spec=pltpu.PrefetchScalarGridSpec(
            num_scalar_prefetch=1,
            grid=(quarter // chunk,),
            in_specs=[pl.BlockSpec((64, WIDTH), lambda n, slot: (0, 0))] * SECTIONS
            + [
                pl.BlockSpec((256, 256), lambda n, slot: (0, 0)),
                pl.BlockSpec((256, chunk), lambda n, slot: (0, n)),
                pl.BlockSpec((256, chunk), lambda n, slot: (0, n)),
            ],
            out_specs=pl.BlockSpec((CHIPS, 16, chunk), lambda n, slot: (0, 0, n)),
            scratch_shapes=[pltpu.VMEM((256, WIDTH), BF16)],
        ),
        out_shape=jax.ShapeDtypeStruct((CHIPS, 16, quarter), BF16),
        compiler_params=pltpu.CompilerParams(vmem_limit_bytes=24 * 2**20),
        cost_estimate=pl.CostEstimate(
            flops=2 * 256 * WIDTH * quarter, bytes_accessed=4 * 2**20, transcendentals=0
        ),
        name="output_terms",
    )(slot, *gathered, order, wo_mine, wo_other)


def body(
    token_ids,
    embedding,
    norm_gain,
    query_weight,
    keyval_weight,
    output_weight,
    prefix_cache,
    prefix_lengths,
):
    section_pos = lax.axis_index("section")
    tensor_pos = lax.axis_index("tensor")
    core, chip = tensor_pos % CORES, tensor_pos // CORES
    quarter = query_weight.shape[1] // SECTIONS

    def own(array, axis, size, distance):
        start = (section_pos + distance) % SECTIONS * size
        return lax.dynamic_slice_in_dim(array, start, size, axis)

    def share(array, axis, size, distance):
        return section_send(own(array, axis, size, distance), distance)

    distances = range(SECTIONS)
    kv_mine = [share(keyval_weight[0].T, 1, quarter, d) for d in distances]
    wq_mine = [share(query_weight[0], 0, quarter, d) if d != 2 else None for d in distances]
    hidden, gains, lengths, (kv_mine, (wq_mine[1], wq_mine[3])) = embed(
        token_ids,
        embedding,
        prefix_lengths,
        norm_gain,
        (kv_mine, (wq_mine[1], wq_mine[3])),
        section_pos,
        core,
    )
    kv_mine = jnp.stack(kv_mine)
    first = chip_send(kv_mine, lambda p: 2 * p if p < 8 else 2 * (p - 8) + 1)
    second = chip_send(kv_mine, lambda p: 2 * p + 1 if p < 8 else 2 * (p - 8))
    rows_first = prefix_cache[0].reshape(SECTIONS, 128, -1)
    cached = [own(rows_first, 0, 1, d)[0] for d in distances]
    hidden, cached = lax.optimization_barrier((hidden, cached))
    cached = [section_send(piece, d) for d, piece in enumerate(cached)]

    def gather_rows(layer):
        scaled = (hidden * gains[layer]).astype(BF16)
        return plane_exchange(jnp.broadcast_to(scaled[None], (CHIPS, 16, quarter)))

    rows = gather_rows(0)
    rows, cached, first, second, query_mat = lax.optimization_barrier(
        (rows, cached, first, second, query_weight[0])
    )
    wq_mine[2] = share(query_mat, 0, quarter, 2)
    cache = plane_exchange(by_head(cached))
    wq_mine, output_mat = lax.optimization_barrier((wq_mine, output_weight[0]))
    wo_mine = [share(output_mat, 1, quarter, d) for d in distances]
    wq_other = jnp.stack([core_swap(w) for w in wq_mine])
    wq_mine = jnp.stack(wq_mine)
    wq_mine, wq_other = lax.optimization_barrier((wq_mine, wq_other))
    even = chip % 2 == 0
    heads_t = []
    for half in (jnp.where(even, first, second), jnp.where(even, second, first)):
        other = core_swap(half)
        low = jnp.where(core == 0, half, other)
        high = jnp.where(core == 0, other, half)
        heads_t.append(jnp.concatenate([low, high], axis=1))
    keys_t, values_t = heads_t

    frequency = ROPE_BASE ** (-(jnp.arange(HD // 2, dtype=F32) * 2.0 / HD))
    positions = (lengths[:, None] + jnp.arange(STEPS)[None, :]).reshape(-1).astype(F32)
    angles = positions[:, None] * frequency[None, :]
    cosine = jnp.concatenate([jnp.cos(angles)] * 2, axis=-1)
    sine = jnp.concatenate([jnp.sin(angles)] * 2, axis=-1)
    row, column = jnp.arange(64)[:, None], jnp.arange(512)[None, :]
    live = jnp.repeat(lengths, STEPS)[:, None]
    live = (row % 16 // 4 == column // 128) & (column % 128 < live)
    bias = jnp.where(live, 0.0, -1e30).astype(F32)
    forward, backward = row_orders(section_pos)

    for layer in range(SECTIONS):
        slot = ((section_pos - layer) % SECTIONS).reshape(1)
        pick = lambda held: lax.dynamic_index_in_dim(held, slot[0], 0, keepdims=False)
        if layer > 0:
            rows = gather_rows(layer)
        weights = [pick(w) for w in (wq_mine, wq_other, keys_t, values_t)]
        partial = project(rows, forward, gains, layer, slot, *weights)
        if layer == 0:
            partial, cache = lax.optimization_barrier((partial, cache))
        parts = section_exchange(partial)
        if layer == 0:
            parts, wo_mine = lax.optimization_barrier((parts, wo_mine))
            wo_other = jnp.stack([core_swap(w) for w in wo_mine])
            wo_mine = jnp.stack(wo_mine)
        mixed = attend(parts, cosine, sine, bias, cache, slot)
        gathered = [section_send(mixed, d) for d in distances]
        terms = plane_exchange(
            output_terms(gathered, backward, slot, pick(wo_mine), pick(wo_other))
        )
        hidden = hidden + jnp.sum(terms.astype(F32), axis=0)

    finals = section_exchange(hidden.reshape(4, STEPS, quarter).transpose(1, 0, 2))
    return finals.transpose(1, 0, 2).reshape(1, 4, SECTIONS * quarter)


def solution(mesh):
    in_specs = (
        P(),
        P("section", "tensor"),
        P("section", None),
        P("section", None, "tensor"),
        P("section", None, "tensor"),
        P("section", "tensor", None),
        P("section", "tensor", None, None, None),
        P("tensor"),
    )
    out_specs = P("section", "tensor", None)
    return jax.shard_map(body, mesh=mesh, in_specs=in_specs, out_specs=out_specs, check_vma=False)
```

```python
import jax
import jax.numpy as jnp
from jax import lax
from jax.experimental import pallas as pl
from jax.experimental.pallas import tpu as pltpu
from jax.sharding import PartitionSpec as P

HD = 128
NORM_EPSILON = 1e-05
ROPE_BASE = 500000.0
SECTIONS = 4
CHIPS = 16
CORES = 2
STEPS = 4
HEADS_PER_CHIP = 4
BF16 = jnp.bfloat16
F32 = jnp.float32
PLANE = [[2 * p + c for p in range(CHIPS)] for c in range(CORES)]


def section_send(block, distance):
    if distance == 0:
        return block
    route = [(i, (i + distance) % SECTIONS) for i in range(SECTIONS)]
    return lax.ppermute(block, "section", route)


def core_swap(block):
    return lax.ppermute(block, "tensor", [(i, i ^ 1) for i in range(CHIPS * CORES)])


def chip_send(block, target):
    route = [(2 * p + c, 2 * target(p) + c) for p in range(CHIPS) for c in range(CORES)]
    return lax.ppermute(block, "tensor", route)


def plane_exchange(blocks):
    return lax.all_to_all(
        blocks, "tensor", split_axis=0, concat_axis=0, tiled=True, axis_index_groups=PLANE
    )


def section_exchange(blocks):
    return lax.all_to_all(blocks, "section", split_axis=0, concat_axis=0, tiled=True)


def in_three(values):
    high = lax.reduce_precision(values, 8, 7)
    middle = lax.reduce_precision(values - high, 8, 7)
    return [part.astype(BF16) for part in (high, middle, values - high - middle)]


def embed(token_ids, embedding, prefix_lengths, norm_gain, early, section_pos, core):
    vocab_part, width = embedding.shape
    local_ids = token_ids.T.reshape(-1) - section_pos * vocab_part
    inside = (local_ids >= 0) & (local_ids < vocab_part)
    picked = jnp.take(embedding, jnp.clip(local_ids, 0, vocab_part - 1), axis=0)
    picked = jnp.where(inside[:, None], picked, jnp.zeros_like(picked))
    picked = picked.reshape(CHIPS * CORES, 16, width)
    extra = jnp.pad(prefix_lengths.astype(BF16)[None, :], ((0, 7), (0, width - 4)))
    extra = jnp.broadcast_to(extra[None], (CHIPS * CORES, 8, width))
    picked = jnp.concatenate([picked, extra], axis=1)
    kv_mine, wq_mine = early
    picked, kv_mine = lax.optimization_barrier((picked, kv_mine))
    by_row = lax.all_to_all(picked, "tensor", split_axis=0, concat_axis=0, tiled=True)
    by_row, wq_mine = lax.optimization_barrier((by_row, wq_mine))
    lengths = by_row[:, 16, :4].reshape(CHIPS, CORES, 4)
    lengths = lax.dynamic_index_in_dim(lengths, core, 1, keepdims=False)
    lengths = lax.dynamic_index_in_dim(lengths, section_pos, 1, keepdims=False)
    gains = jnp.stack(in_three(norm_gain.reshape(CHIPS * CORES, width)), axis=1)
    gains = jnp.pad(gains, ((0, 0), (0, 5), (0, 0)))
    by_quarter = section_exchange(jnp.concatenate([by_row[:, :16], gains], axis=1))
    by_quarter = by_quarter.reshape(SECTIONS, 8, 24, width).astype(F32)
    columns = jnp.sum(by_quarter[:, :, :16], axis=0).transpose(1, 0, 2).reshape(16, -1)
    gains = (by_quarter[:, :, 16] + by_quarter[:, :, 17]) + by_quarter[:, :, 18]
    return columns, gains.reshape(SECTIONS, 1, -1), lengths.astype(jnp.int32), (kv_mine, wq_mine)


def row_orders(section_pos):
    place = jnp.arange(256)[:, None]
    source = jnp.arange(256)[None, :]
    wanted = place // 4 % CHIPS * 16 + place // 64 * 4 + place % 4
    forward = (wanted == source).astype(BF16)
    held = source // 4 % CHIPS * 16 + (section_pos - source // 64) % SECTIONS * 4 + source % 4
    backward = (held == place).astype(BF16)
    return forward, backward


TRANSPOSED = (((1,), (1,)), ((), ()))
WIDTH = HEADS_PER_CHIP * HD
SENT = WIDTH + 3 * HD


def by_head_kernel(first, second, third, fourth, out):
    for d, piece in enumerate((first, second, third, fourth)):
        for p in range(CHIPS):
            for i in range(2):
                start = 1024 * i + HD * (p // 2)
                out[p, d, i] = piece[:, start : start + HD]


def by_head(pieces):
    whole = pl.BlockSpec(pieces[0].shape, lambda i: (0, 0))
    shape = (CHIPS, SECTIONS, 2, 128, HD)
    return pl.pallas_call(
        by_head_kernel,
        grid=(1,),
        in_specs=[whole] * SECTIONS,
        out_specs=pl.BlockSpec(shape, lambda i: (0, 0, 0, 0, 0)),
        out_shape=jax.ShapeDtypeStruct(shape, BF16),
        compiler_params=pltpu.CompilerParams(vmem_limit_bytes=32 * 2**20),
        cost_estimate=pl.CostEstimate(flops=0, bytes_accessed=7 * 2**20, transcendentals=0),
        name="by_head",
    )(*pieces)


def project_kernel(slot, rows, order, gain, wq_mine, wq_other, keys_t, values_t, out, total):
    step = pl.program_id(0)

    @pl.when(step == 0)
    def _():
        total[...] = jnp.zeros_like(total)

    block = rows[...].reshape(256, rows.shape[2])
    block = jnp.dot(order[...], block, preferred_element_type=F32).astype(BF16)
    plain = block.astype(F32) / gain[...]
    half = WIDTH // 2
    total[:, :half] += jnp.dot(block, wq_mine[...], preferred_element_type=F32)
    total[:, half:WIDTH] += jnp.dot(block, wq_other[...], preferred_element_type=F32)
    for start, weight in ((WIDTH, keys_t), (WIDTH + HD, values_t)):
        total[:, start : start + HD] += lax.dot_general(
            block, weight[...], TRANSPOSED, preferred_element_type=F32
        )
    total[:, WIDTH + 2 * HD :] += jnp.sum(plain * plain, axis=1, keepdims=True)

    @pl.when(step == pl.num_programs(0) - 1)
    def _():
        squares = total[:, WIDTH + 2 * HD :]
        high = squares.astype(BF16).astype(F32)
        middle = (squares - high).astype(BF16).astype(F32)
        low = squares - high - middle
        lane = lax.broadcasted_iota(jnp.int32, squares.shape, 1)
        parts = jnp.where(lane == 0, high, jnp.where(lane == 1, middle, low))
        parts = jnp.where(lane < 3, parts, 0.0)
        for j in range(SECTIONS):
            own = slice(64 * j, 64 * (j + 1))
            out[j, :, : WIDTH + 2 * HD] = total[own, : WIDTH + 2 * HD].astype(BF16)
            out[j, :, WIDTH + 2 * HD :] = parts[own].astype(BF16)


def project(rows, order, gain, layer, slot, wq_mine, wq_other, keys_t, values_t):
    quarter = rows.shape[2]
    chunk = quarter // 4
    flops = 2 * 256 * quarter * (256 + WIDTH + 2 * HD)
    return pl.pallas_call(
        project_kernel,
        grid_spec=pltpu.PrefetchScalarGridSpec(
            num_scalar_prefetch=1,
            grid=(quarter // chunk,),
            in_specs=[
                pl.BlockSpec((CHIPS, 16, chunk), lambda k, slot: (0, 0, k)),
                pl.BlockSpec((256, 256), lambda k, slot: (0, 0)),
                pl.BlockSpec((None, 1, chunk), lambda k, slot: (layer, 0, k)),
                pl.BlockSpec((chunk, 256), lambda k, slot: (k, 0)),
                pl.BlockSpec((chunk, 256), lambda k, slot: (k, 0)),
                pl.BlockSpec((HD, chunk), lambda k, slot: (0, k)),
                pl.BlockSpec((HD, chunk), lambda k, slot: (0, k)),
            ],
            out_specs=pl.BlockSpec((SECTIONS, 64, SENT), lambda k, slot: (0, 0, 0)),
            scratch_shapes=[pltpu.VMEM((256, SENT), F32)],
        ),
        out_shape=jax.ShapeDtypeStruct((SECTIONS, 64, SENT), BF16),
        compiler_params=pltpu.CompilerParams(vmem_limit_bytes=24 * 2**20),
        cost_estimate=pl.CostEstimate(flops=flops, bytes_accessed=5 * 2**20, transcendentals=0),
        name="project",
    )(slot, rows, order, gain, wq_mine, wq_other, keys_t, values_t)


def attend_kernel(slot, parts, cosine, sine, bias, cache, out):
    total = parts[0].astype(F32)
    for i in range(1, SECTIONS):
        total = total + parts[i].astype(F32)
    squares = jnp.sum(total[:, WIDTH + 2 * HD :], axis=1, keepdims=True)
    scaling = lax.rsqrt(squares / 8192.0 + NORM_EPSILON)
    turned_cos = cosine[...] * scaling
    turned_sin = sine[...] * scaling

    def turn(vectors):
        half = HD // 2
        swapped = jnp.concatenate([-vectors[:, half:], vectors[:, :half]], axis=1)
        return (vectors * turned_cos + swapped * turned_sin).astype(BF16)

    queries = [turn(total[:, HD * h : HD * (h + 1)]) for h in range(HEADS_PER_CHIP)]
    new_keys = turn(total[:, WIDTH : WIDTH + HD])
    new_values = (total[:, WIDTH + HD : WIDTH + 2 * HD] * scaling).astype(BF16)
    row = lax.broadcasted_iota(jnp.int32, (64, 16), 0) % 16
    column = lax.broadcasted_iota(jnp.int32, (64, 16), 1)
    new_live = (row // 4 == column // 4) & (column % 4 <= row % 4)
    scale = HD**-0.5
    for g in range(4):
        own = slice(16 * g, 16 * (g + 1))
        query = jnp.concatenate([q[own] for q in queries], axis=0)
        keys = cache[4 * g : 4 * (g + 1), 0].reshape(4 * 128, HD)
        values = cache[4 * g : 4 * (g + 1), 1].reshape(4 * 128, HD)
        past = lax.dot_general(query, keys, TRANSPOSED, preferred_element_type=F32) * scale
        new = lax.dot_general(query, new_keys[own], TRANSPOSED, preferred_element_type=F32) * scale
        past = past + jnp.concatenate([bias[own]] * HEADS_PER_CHIP, axis=0)
        new = jnp.where(new_live, new, -1e30)
        top = jnp.maximum(
            jnp.max(past, axis=1, keepdims=True), jnp.max(new, axis=1, keepdims=True)
        )
        past = jnp.exp(past - top)
        new = jnp.exp(new - top)
        weight = jnp.sum(past, axis=1, keepdims=True) + jnp.sum(new, axis=1, keepdims=True)
        past = (past / weight).astype(BF16)
        new = (new / weight).astype(BF16)
        mixed = jnp.dot(past, values, preferred_element_type=F32)
        mixed = mixed + jnp.dot(new, new_values[own], preferred_element_type=F32)
        mixed = mixed.astype(BF16)
        for h in range(HEADS_PER_CHIP):
            out[own, HD * h : HD * (h + 1)] = mixed[16 * h : 16 * (h + 1)]


def attend(parts, cosine, sine, bias, cache, slot):
    whole = lambda *shape: pl.BlockSpec(shape, lambda i, slot: (0,) * len(shape))
    return pl.pallas_call(
        attend_kernel,
        grid_spec=pltpu.PrefetchScalarGridSpec(
            num_scalar_prefetch=1,
            grid=(1,),
            in_specs=[
                whole(SECTIONS, 64, SENT),
                whole(64, HD),
                whole(64, HD),
                whole(64, 512),
                pl.BlockSpec((CHIPS, None, 2, 128, HD), lambda i, slot: (0, slot[0], 0, 0, 0)),
            ],
            out_specs=whole(64, WIDTH),
        ),
        out_shape=jax.ShapeDtypeStruct((64, WIDTH), BF16),
        compiler_params=pltpu.CompilerParams(vmem_limit_bytes=32 * 2**20),
        cost_estimate=pl.CostEstimate(
            flops=2**28, bytes_accessed=2 * 2**20, transcendentals=2**17
        ),
        name="attend",
    )(slot, parts, cosine, sine, bias, cache)


def output_kernel(slot, first, second, third, fourth, order, wo_mine, wo_other, out, ordered):
    @pl.when(pl.program_id(0) == 0)
    def _():
        mixed = jnp.concatenate([first[...], second[...], third[...], fourth[...]], axis=0)
        ordered[...] = jnp.dot(order[...], mixed, preferred_element_type=F32).astype(BF16)

    half = WIDTH // 2
    terms = jnp.dot(ordered[:, :half], wo_mine[...], preferred_element_type=F32)
    terms = terms + jnp.dot(ordered[:, half:], wo_other[...], preferred_element_type=F32)
    out[...] = terms.astype(BF16).reshape(out.shape)


def output_terms(gathered, order, slot, wo_mine, wo_other):
    quarter = wo_mine.shape[1]
    chunk = quarter // 4
    return pl.pallas_call(
        output_kernel,
        grid_spec=pltpu.PrefetchScalarGridSpec(
            num_scalar_prefetch=1,
            grid=(quarter // chunk,),
            in_specs=[pl.BlockSpec((64, WIDTH), lambda n, slot: (0, 0))] * SECTIONS
            + [
                pl.BlockSpec((256, 256), lambda n, slot: (0, 0)),
                pl.BlockSpec((256, chunk), lambda n, slot: (0, n)),
                pl.BlockSpec((256, chunk), lambda n, slot: (0, n)),
            ],
            out_specs=pl.BlockSpec((CHIPS, 16, chunk), lambda n, slot: (0, 0, n)),
            scratch_shapes=[pltpu.VMEM((256, WIDTH), BF16)],
        ),
        out_shape=jax.ShapeDtypeStruct((CHIPS, 16, quarter), BF16),
        compiler_params=pltpu.CompilerParams(vmem_limit_bytes=24 * 2**20),
        cost_estimate=pl.CostEstimate(
            flops=2 * 256 * WIDTH * quarter, bytes_accessed=4 * 2**20, transcendentals=0
        ),
        name="output_terms",
    )(slot, *gathered, order, wo_mine, wo_other)


def body(
    token_ids,
    embedding,
    norm_gain,
    query_weight,
    keyval_weight,
    output_weight,
    prefix_cache,
    prefix_lengths,
):
    section_pos = lax.axis_index("section")
    tensor_pos = lax.axis_index("tensor")
    core, chip = tensor_pos % CORES, tensor_pos // CORES
    quarter = query_weight.shape[1] // SECTIONS

    def own(array, axis, size, distance):
        start = (section_pos + distance) % SECTIONS * size
        return lax.dynamic_slice_in_dim(array, start, size, axis)

    def share(array, axis, size, distance):
        return section_send(own(array, axis, size, distance), distance)

    distances = range(SECTIONS)
    kv_mine = [share(keyval_weight[0].T, 1, quarter, d) for d in distances]
    wq_mine = [share(query_weight[0], 0, quarter, d) if d != 2 else None for d in distances]
    hidden, gains, lengths, (kv_mine, (wq_mine[1], wq_mine[3])) = embed(
        token_ids,
        embedding,
        prefix_lengths,
        norm_gain,
        (kv_mine, (wq_mine[1], wq_mine[3])),
        section_pos,
        core,
    )
    kv_mine = jnp.stack(kv_mine)
    first = chip_send(kv_mine, lambda p: 2 * p if p < 8 else 2 * (p - 8) + 1)
    second = chip_send(kv_mine, lambda p: 2 * p + 1 if p < 8 else 2 * (p - 8))
    rows_first = prefix_cache[0].reshape(SECTIONS, 128, -1)
    cached = [own(rows_first, 0, 1, d)[0] for d in distances]
    hidden, cached = lax.optimization_barrier((hidden, cached))
    cached = [section_send(piece, d) for d, piece in enumerate(cached)]

    def gather_rows(layer):
        scaled = (hidden * gains[layer]).astype(BF16)
        return plane_exchange(jnp.broadcast_to(scaled[None], (CHIPS, 16, quarter)))

    rows = gather_rows(0)
    rows, cached, first, second, query_mat = lax.optimization_barrier(
        (rows, cached, first, second, query_weight[0])
    )
    wq_mine[2] = share(query_mat, 0, quarter, 2)
    cache = plane_exchange(by_head(cached))
    wq_mine, output_mat = lax.optimization_barrier((wq_mine, output_weight[0]))
    wo_mine = [share(output_mat, 1, quarter, d) if d != 2 else None for d in distances]
    wq_other = jnp.stack([core_swap(w) for w in wq_mine])
    wq_mine = jnp.stack(wq_mine)
    wq_mine, wq_other = lax.optimization_barrier((wq_mine, wq_other))
    even = chip % 2 == 0
    heads_t = []
    for half in (jnp.where(even, first, second), jnp.where(even, second, first)):
        other = core_swap(half)
        low = jnp.where(core == 0, half, other)
        high = jnp.where(core == 0, other, half)
        heads_t.append(jnp.concatenate([low, high], axis=1))
    keys_t, values_t = heads_t

    frequency = ROPE_BASE ** (-(jnp.arange(HD // 2, dtype=F32) * 2.0 / HD))
    positions = (lengths[:, None] + jnp.arange(STEPS)[None, :]).reshape(-1).astype(F32)
    angles = positions[:, None] * frequency[None, :]
    cosine = jnp.concatenate([jnp.cos(angles)] * 2, axis=-1)
    sine = jnp.concatenate([jnp.sin(angles)] * 2, axis=-1)
    row, column = jnp.arange(64)[:, None], jnp.arange(512)[None, :]
    live = jnp.repeat(lengths, STEPS)[:, None]
    live = (row % 16 // 4 == column // 128) & (column % 128 < live)
    bias = jnp.where(live, 0.0, -1e30).astype(F32)
    forward, backward = row_orders(section_pos)

    for layer in range(SECTIONS):
        slot = ((section_pos - layer) % SECTIONS).reshape(1)
        pick = lambda held: lax.dynamic_index_in_dim(held, slot[0], 0, keepdims=False)
        if layer > 0:
            rows = gather_rows(layer)
        weights = [pick(w) for w in (wq_mine, wq_other, keys_t, values_t)]
        partial = project(rows, forward, gains, layer, slot, *weights)
        if layer == 0:
            partial, cache, output_mat = lax.optimization_barrier((partial, cache, output_mat))
            wo_mine[2] = share(output_mat, 1, quarter, 2)
        parts = section_exchange(partial)
        if layer == 0:
            parts, wo_mine[1], wo_mine[3] = lax.optimization_barrier(
                (parts, wo_mine[1], wo_mine[3])
            )
            wo_other = jnp.stack([core_swap(w) for w in wo_mine])
            wo_mine = jnp.stack(wo_mine)
        mixed = attend(parts, cosine, sine, bias, cache, slot)
        gathered = [section_send(mixed, d) for d in distances]
        terms = plane_exchange(
            output_terms(gathered, backward, slot, pick(wo_mine), pick(wo_other))
        )
        hidden = hidden + jnp.sum(terms.astype(F32), axis=0)

    finals = section_exchange(hidden.reshape(4, STEPS, quarter).transpose(1, 0, 2))
    return finals.transpose(1, 0, 2).reshape(1, 4, SECTIONS * quarter)


def solution(mesh):
    in_specs = (
        P(),
        P("section", "tensor"),
        P("section", None),
        P("section", None, "tensor"),
        P("section", None, "tensor"),
        P("section", "tensor", None),
        P("section", "tensor", None, None, None),
        P("tensor"),
    )
    out_specs = P("section", "tensor", None)
    return jax.shard_map(body, mesh=mesh, in_specs=in_specs, out_specs=out_specs, check_vma=False)
```
